32 devices in a mesh: row: 4 (over x, core), col: 8 (over z, y).
Axes of the slice: x: 2, y: 2, z: 4, core: 2. Of those that a mesh axis runs over, the one named last changes fastest.
Arguments:
- panel_inverse: bfloat16 [2, 2, 2, 1024, 1024], P(None, None, None, ('row', 'col')), may hold values from -0.125 to 0.125
- panel_below: bfloat16 [2, 2, 1024, 1024], P(None, None, ('row', 'col')), may hold values from -0.25 to 0.25
- trail_factor: bfloat16 [2, 2, 2, 32768, 1024], P(None, None, None, ('row', 'col')), may hold values from -0.125 to 0.125
- first_rhs: bfloat16 [2, 2, 1024, 256], replicated, may hold values from -6 to 6
- second_rhs: bfloat16 [2, 2, 1024, 256], P(None, None, ('row', 'col')), may hold values from -6 to 6
- trail_rhs: bfloat16 [2, 2, 32768, 256], P(None, None, ('row', 'col')), may hold values from -6 to 6
- shape_tiles: float32 [2, 9, 2, 1024], P(None, None, None, ('row', 'col')), may hold values from -0.25 to 0.25
- element_vertices: int32 [2, 1024, 3], P(None, ('row', 'col')), may hold values from 0 to 255, all different within a row
- vertex_slot: int32 [256], replicated, may hold values from 0 to 255, each once
Outputs:
- panel_solution: bfloat16 [2, 2, 2, 1024, 256], P(None, None, None, ('row', 'col'))
- trail_update: bfloat16 [2, 2, 32768, 256], P(None, None, ('row', 'col'))
- vertex_gradient: float32 [3, 256], P(None, ('row', 'col'))
The draws below stay inside these ranges and needn't reach their ends.
Inputs may be any that keep to these rules, and one draw needn't show every extreme that they name: `element_vertices`: each element names three different vertices, and every vertex is named by some element. `vertex_slot`: each slot is given to exactly one vertex.
All inputs are finite; a program needn't handle non-finite values.
Results may differ from the reference program's by a relative error of at most 0.0067.
Values may be sent and summed in bfloat16 or wider, within the bound.
A program may use at most 128 MiB of HBM per device.

```python
import jax
import jax.numpy as jnp
from jax import lax

NB = 1024
ANG = 256
ORDER = 32768
NV = 256


def raised(drawn, stream_key, source, target, blocks, factor):
    owner, partner = [(jnp.arange(drawn.shape[position]) // (drawn.shape[position] // blocks)).reshape([-1 if axis == position else 1 for axis in range(drawn.ndim)]) for position in (source, target)]
    chosen = jax.random.permutation(stream_key, blocks)[partner]
    strong = (owner == chosen) | (owner == (partner + blocks // 2) % blocks)
    return jnp.where(strong, factor * drawn, drawn)


def block_levels(rng, extent, pieces, smallest, high):
    def one(axis_at, parts):
        draws = jax.random.uniform(jax.random.fold_in(jax.random.fold_in(rng, 6), axis_at), (parts,), jnp.float32, smallest / len(pieces), high / len(pieces))
        return jnp.repeat(jnp.exp(draws), extent[axis_at] // parts).reshape((-1,) + (1,) * (len(extent) - axis_at - 1))

    loudness = one(*pieces[0])
    for cut in pieces[1:]:
        loudness = loudness * one(*cut)
    return loudness


def picks_of(key, rows, number_of, top, lift):
    ranking = jax.random.permutation(jax.random.fold_in(key, 1), number_of)
    boost = ranking
    for power in range(3):
        boost = boost * boost // number_of
    boost = boost * lift // number_of
    lots = jax.random.randint(jax.random.fold_in(key, 2), (rows, number_of), 0, 4096) + boost
    fixed_rows = jax.random.permutation(jax.random.fold_in(key, 3), rows)[jnp.arange(number_of) % rows]
    lots = jnp.where(jnp.arange(rows)[:, None] == fixed_rows[None, :], 1 << 14, lots)
    merit = lots * number_of + jnp.arange(number_of)
    return lax.top_k(merit.astype(jnp.int32), top)[1].astype(jnp.int32)


def bell_draw(own_key, shape, spread, bound, shards=(), kind=jnp.bfloat16):
    loudness = block_levels(own_key, shape, shards, -0.22, 0.18) if shards else 1.0
    entries = jax.random.normal(own_key, shape, jnp.float32) * spread * loudness
    return jnp.minimum(jnp.maximum(entries, -bound), bound).astype(kind)


def noise_with(key, shape, width, bound, shards, heavy, dtype=jnp.bfloat16):
    drawn = width * jax.random.normal(key, shape, jnp.float32)
    if shards:
        drawn = drawn * block_levels(key, shape, shards, -0.22, 0.18)
    return jnp.clip(raised(drawn, jax.random.fold_in(key, 3), *heavy), -bound, bound).astype(dtype)


def setup_inputs(seed: int = 0) -> dict:
    key_list = jax.random.split(jax.random.key(seed), 10)
    panel_inverse = bell_draw(key_list[0], (2, 2, 2, NB, NB), (2 * NB) ** -0.5, 0.125, ((3, 32),))
    panel_below = noise_with(key_list[1], (2, 2, NB, NB), (2 * NB) ** -0.5, 0.25, ((2, 32),), (2, 3, 32, 2.75))
    trail_factor = bell_draw(key_list[2], (2, 2, 2, ORDER, NB), (2 * NB) ** -0.5, 0.125, ((3, 32),))
    first_rhs = bell_draw(key_list[3], (2, 2, NB, ANG), 1.0, 6.0)
    second_rhs = bell_draw(key_list[4], (2, 2, NB, ANG), 1.0, 6.0, ((2, 32),))
    trail_rhs = bell_draw(key_list[5], (2, 2, ORDER, ANG), 1.0, 6.0, ((2, 32),))
    shape_tiles = bell_draw(key_list[6], (2, 9, 2, NB), (0.25 * ANG ** -0.5), 0.25, ((3, 32),), jnp.float32)
    element_vertices = picks_of(key_list[7], 2 * NB, NV, 3, 192).reshape((2, NB, 3))
    vertex_slot = jax.random.permutation(key_list[8], NV).astype(jnp.int32)
    return dict(panel_inverse=panel_inverse, panel_below=panel_below, trail_factor=trail_factor, first_rhs=first_rhs, second_rhs=second_rhs, trail_rhs=trail_rhs, shape_tiles=shape_tiles, element_vertices=element_vertices, vertex_slot=vertex_slot)


def complex_dot(left_real, left_imag, right_real, right_imag):
    left_real = left_real.astype(jnp.float32)
    left_imag = left_imag.astype(jnp.float32)
    right_real = right_real.astype(jnp.float32)
    right_imag = right_imag.astype(jnp.float32)
    real_part = jnp.dot(left_real, right_real, preferred_element_type=jnp.float32) - jnp.dot(left_imag, right_imag, preferred_element_type=jnp.float32)
    imag_part = jnp.dot(left_real, right_imag, preferred_element_type=jnp.float32) + jnp.dot(left_imag, right_real, preferred_element_type=jnp.float32)
    return real_part, imag_part


def couple_partials(panel_solution, shape_tiles):
    forward = panel_solution[0].astype(jnp.float32)
    adjoint = panel_solution[1].astype(jnp.float32)
    coupling_real = jnp.sum(forward[:, 0] * adjoint[:, 0] - forward[:, 1] * adjoint[:, 1], axis=-1)
    coupling_imag = jnp.sum(forward[:, 0] * adjoint[:, 1] + forward[:, 1] * adjoint[:, 0], axis=-1)
    return -(shape_tiles[0] * coupling_real - shape_tiles[1] * coupling_imag)


def spread_vertices(partials, element_vertices, vertex_slot, vertex_count):
    values = jnp.transpose(partials.reshape(3, 3, partials.shape[1], partials.shape[2]), (1, 2, 3, 0))
    slots = vertex_slot[element_vertices].astype(jnp.int32)
    empty = jnp.zeros((3, vertex_count), jnp.float32)
    return empty.at[:, slots.reshape(-1)].add(values.reshape(3, -1))


def reference(panel_inverse, panel_below, trail_factor, first_rhs, second_rhs, trail_rhs, shape_tiles, element_vertices, vertex_slot):
    solutions = []
    updates = []
    for system in range(2):
        inverse = panel_inverse[system]
        first_real, first_imag = complex_dot(inverse[0, 0], inverse[0, 1], first_rhs[system, 0], first_rhs[system, 1])
        first_real = first_real.astype(jnp.bfloat16)
        first_imag = first_imag.astype(jnp.bfloat16)
        below_real, below_imag = complex_dot(panel_below[system, 0].T, panel_below[system, 1].T, first_real, first_imag)
        right_real = (second_rhs[system, 0].astype(jnp.float32) - below_real).astype(jnp.bfloat16)
        right_imag = (second_rhs[system, 1].astype(jnp.float32) - below_imag).astype(jnp.bfloat16)
        second_real, second_imag = complex_dot(inverse[1, 0], inverse[1, 1], right_real, right_imag)
        second_real = second_real.astype(jnp.bfloat16)
        second_imag = second_imag.astype(jnp.bfloat16)
        update_real = trail_rhs[system, 0].astype(jnp.float32)
        update_imag = trail_rhs[system, 1].astype(jnp.float32)
        pairs = ((first_real, first_imag), (second_real, second_imag))
        for section_index in range(2):
            term_real, term_imag = complex_dot(trail_factor[system, section_index, 0], trail_factor[system, section_index, 1], pairs[section_index][0], pairs[section_index][1])
            update_real = update_real - term_real
            update_imag = update_imag - term_imag
        updates.append(jnp.stack([update_real, update_imag]).astype(jnp.bfloat16))
        solutions.append(jnp.stack([jnp.stack([first_real, first_imag]), jnp.stack([second_real, second_imag])]))
    panel_solution = jnp.stack(solutions)
    trail_update = jnp.stack(updates)
    partials = couple_partials(panel_solution, shape_tiles)
    vertex_gradient = spread_vertices(partials, element_vertices, vertex_slot, NV)
    return panel_solution, trail_update, vertex_gradient
```

```python
import functools

import jax
import jax.numpy as jnp
from jax import lax
from jax.experimental import pallas as pl
from jax.experimental.pallas import tpu as pltpu
from jax.sharding import PartitionSpec as P

MESH = pl.DeviceIdType.MESH
F32 = jnp.float32
BF16 = jnp.bfloat16


def couple_partials(panel_solution, shape_tiles):
    forward = panel_solution[0].astype(jnp.float32)
    adjoint = panel_solution[1].astype(jnp.float32)
    coupling_real = jnp.sum(forward[:, 0] * adjoint[:, 0] - forward[:, 1] * adjoint[:, 1], axis=-1)
    coupling_imag = jnp.sum(forward[:, 0] * adjoint[:, 1] + forward[:, 1] * adjoint[:, 0], axis=-1)
    return -(shape_tiles[0] * coupling_real - shape_tiles[1] * coupling_imag)


def spread_vertices(partials, element_vertices, vertex_slot, vertex_count):
    values = jnp.transpose(
        partials.reshape(3, 3, partials.shape[1], partials.shape[2]), (1, 2, 3, 0)
    )
    slots = vertex_slot[element_vertices]
    empty = jnp.zeros((3, vertex_count), jnp.float32)
    return empty.at[:, slots.reshape(-1)].add(values.reshape(3, -1))


def stack_rows(top, bottom):
    if top.shape[0] % 16:
        return jnp.concatenate([top.astype(F32), bottom.astype(F32)], axis=0).astype(BF16)
    return jnp.concatenate([top, bottom], axis=0)


def kernel(dims, inv, below, second, rhs_hbm, factor_hbm, trail_hbm, panel_out, update_hbm,
           rhs, factor, trail, update, held, columns,
           rhs_sem, factor_sem, trail_sem, update_sem,
           sems, column_send, column_recv):
    nx, ny, nz = dims
    rows, cols = nx * 2, ny * nz
    n = rows * cols
    h = inv.shape[3]
    nb = inv.shape[4]
    angles = second.shape[3]
    steps = factor.shape[3] // trail_tile(factor.shape[3])
    tile = trail_tile(factor.shape[3])
    row, col = lax.axis_index("row"), lax.axis_index("col")
    x, core = row // 2, row % 2
    z, y = col // ny, col % ny
    me = row * cols + col
    sent = []

    loads = {}
    for s in range(2):
        loads["rhs", s] = pltpu.make_async_copy(rhs_hbm.at[s], rhs.at[s], rhs_sem.at[s])
        loads["rhs", s].start()

    barrier = pltpu.get_barrier_semaphore()

    def greet(k, carry):
        other = lax.rem(me + k, n)
        pl.semaphore_signal(barrier, inc=1, device_id=(other // cols, other % cols),
                            device_id_type=MESH)
        return carry

    lax.fori_loop(1, n, greet, 0)
    for t in range(2):
        for s in range(2):
            loads["factor", s, t] = pltpu.make_async_copy(
                factor_hbm.at[s, t], factor.at[s, t], factor_sem.at[s, t])
            loads["factor", s, t].start()
            if t == 0:
                loads["trail", s] = pltpu.make_async_copy(
                    trail_hbm.at[s], trail.at[s], trail_sem.at[s])
                loads["trail", s].start()

    def column_copy(target, source):
        return pltpu.make_async_remote_copy(
            src_ref=below.at[target], dst_ref=columns.at[source],
            send_sem=column_send.at[target], recv_sem=column_recv.at[source],
            device_id=(target // cols, target % cols), device_id_type=MESH)

    def remote(index, stage, k, region, target):
        copy = pltpu.make_async_remote_copy(
            src_ref=held.at[(index,) + region], dst_ref=held.at[(index,) + region],
            send_sem=sems.at[0, stage, index, k], recv_sem=sems.at[1, stage, index, k],
            device_id=target, device_id_type=MESH)
        return copy

    def send(index, stage, k, region, target):
        copy = remote(index, stage, k, region, target)
        copy.start()
        sent.append(copy)

    def receive(index, stage, k, region):
        remote(index, stage, k, region, (row, col)).wait_recv()

    every = slice(None)

    def spread(round_, s, make_block):
        indices = [(round_ * 2 + s) * 2 + p for p in range(2)]
        mate = (x * 2 + 1 - core, col)
        real, imag = make_block()
        for i, part in zip(indices, (real, imag)):
            held[i, x, core, z, y] = part.astype(held.dtype)
            for k in range(1, nz):
                send(i, 0, k, (x, core, z, y), (row, lax.rem(z + k, nz) * ny + y))
        yield
        for p, i in enumerate(indices):
            for k in range(1, nz):
                receive(i, 0, k, (x, core, lax.rem(z + nz - k, nz), y))
            line = (x, core, every, y)
            if p == 0:
                for k in range(1, ny):
                    send(i, 1, k, line, (row, z * ny + lax.rem(y + k, ny)))
            else:
                for k in range(1, nx):
                    send(i, 1, k, line, (lax.rem(x + k, nx) * 2 + core, col))
            send(i, 3, 0, line, mate)
        yield
        for p, i in enumerate(indices):
            if p == 0:
                got = [(x, core, every, lax.rem(y + ny - k, ny)) for k in range(1, ny)]
            else:
                got = [(lax.rem(x + nx - k, nx), core, every, y) for k in range(1, nx)]
            for k, region in enumerate(got):
                receive(i, 1, k + 1, region)
            if p == 0:
                for k in range(1, nx):
                    send(i, 2, k, (x, core), (lax.rem(x + k, nx) * 2 + core, col))
            else:
                for k in range(1, ny):
                    send(i, 2, k, (every, core, every, y), (row, z * ny + lax.rem(y + k, ny)))
            for k, region in enumerate(got):
                send(i, 3, 1 + k, region, mate)
        yield
        for p, i in enumerate(indices):
            if p == 0:
                got = [(lax.rem(x + nx - k, nx), core) for k in range(1, nx)]
            else:
                got = [(every, core, every, lax.rem(y + ny - k, ny)) for k in range(1, ny)]
            for k, region in enumerate(got):
                receive(i, 2, k + 1, region)
                base = ny if p == 0 else nx
                send(i, 3, base + k, region, mate)
        yield
        far = 1 - core
        for p, i in enumerate(indices):
            receive(i, 3, 0, (x, far, every, y))
            if p == 0:
                got = [(x, far, every, lax.rem(y + ny - k, ny)) for k in range(1, ny)]
                got += [(lax.rem(x + nx - k, nx), far) for k in range(1, nx)]
            else:
                got = [(lax.rem(x + nx - k, nx), far, every, y) for k in range(1, nx)]
                got += [(every, far, every, lax.rem(y + ny - k, ny)) for k in range(1, ny)]
            for k, region in enumerate(got):
                receive(i, 3, 1 + k, region)

    def gathered(round_, s, p):
        block = held[(round_ * 2 + s) * 2 + p]
        return block.reshape(nb, angles).astype(BF16)

    def dot(a, b):
        return jnp.dot(a, b, preferred_element_type=F32)

    def solve(s, panel, right):
        left = stack_rows(inv[s, panel, 0], inv[s, panel, 1])
        by_real, by_imag = dot(left, right[0]), dot(left, right[1])
        real = (by_real[:h] - by_imag[h:]).astype(BF16)
        imag = (by_imag[:h] + by_real[h:]).astype(BF16)
        panel_out[s, panel, 0] = real
        panel_out[s, panel, 1] = imag
        return real, imag

    def first_block(s):
        loads["rhs", s].wait()
        return solve(s, 0, (rhs[s, 0], rhs[s, 1]))

    def right_block(s):
        left = columns[...].astype(BF16).reshape(nb, columns.shape[2])
        products = [lax.dot_general(left, gathered(0, s, p), (((0,), (0,)), ((), ())),
                                    preferred_element_type=F32) for p in range(2)]
        a, b = 2 * s * h, (2 * s + 1) * h
        real = products[0][a:a + h] - products[1][b:b + h]
        imag = products[1][a:a + h] + products[0][b:b + h]
        return (second[s, 0].astype(F32) - real).astype(BF16), (
            second[s, 1].astype(F32) - imag).astype(BF16)

    def second_block(s):
        return solve(s, 1, (gathered(1, s, 0), gathered(1, s, 1)))

    def trail_part(s, t, part):
        at = pl.ds(part * tile, tile)
        solved = [gathered(2 * t, s, p) for p in range(2)]
        fr, fi = factor[s, t, 0, at, :], factor[s, t, 1, at, :]
        real = dot(fr, solved[0]) - dot(fi, solved[1])
        imag = dot(fr, solved[1]) + dot(fi, solved[0])
        if t == 0:
            update[s, 0, at, :] = trail[s, 0, at, :].astype(F32) - real
            update[s, 1, at, :] = trail[s, 1, at, :].astype(F32) - imag
        else:
            trail[s, 0, at, :] = (update[s, 0, at, :] - real).astype(BF16)
            trail[s, 1, at, :] = (update[s, 1, at, :] - imag).astype(BF16)

    def trail_run(s, t, first, last):
        if first == 0:
            loads["factor", s, t].wait()
            if t == 0:
                loads["trail", s].wait()
        for part in range(first, last):
            trail_part(s, t, part)

    def chain(s):
        yield from spread(0, s, lambda: first_block(s))
        yield from spread(1, s, lambda: right_block(s))
        yield from spread(2, s, lambda: second_block(s))

    columns[me] = below[me]
    pl.semaphore_wait(barrier, n - 1)

    chains = [chain(0), chain(1)]
    next(chains[0])
    next(chains[1])

    def scatter(k, carry):
        column_copy(lax.rem(me + k, n), me).start()
        return carry

    lax.fori_loop(1, n, scatter, 0)
    next(chains[0])
    next(chains[1])
    next(chains[0])
    next(chains[1])
    next(chains[0])

    def collect(k, carry):
        column_copy(lax.rem(me + k, n), lax.rem(me + n - k, n)).wait()
        return carry

    lax.fori_loop(1, n, collect, 0)
    half = steps // 2
    next(chains[0])
    next(chains[1])
    next(chains[0])
    next(chains[1])
    trail_run(0, 0, 0, half)
    next(chains[0])
    next(chains[1])
    trail_run(0, 0, half, steps)
    next(chains[0])
    next(chains[1])
    next(chains[0])
    next(chains[1])
    next(chains[0])
    next(chains[1])
    trail_run(1, 0, 0, half)
    next(chains[0])
    next(chains[1])
    trail_run(1, 0, half, steps)
    next(chains[0])
    next(chains[1])
    next(chains[0], None)
    next(chains[1])
    stores = []
    trail_run(0, 1, 0, steps)
    stores.append(pltpu.make_async_copy(trail.at[0], update_hbm.at[0], update_sem.at[0]))
    stores[0].start()
    next(chains[1], None)
    trail_run(1, 1, 0, steps)
    stores.append(pltpu.make_async_copy(trail.at[1], update_hbm.at[1], update_sem.at[1]))
    stores[1].start()
    for copy in sent:
        copy.wait_send()
    for copy in stores:
        copy.wait()


def trail_tile(count):
    return min(count, 256)


def body(dims, panel_inverse, panel_below, trail_factor, first_rhs, second_rhs, trail_rhs,
         shape_tiles, element_vertices, vertex_slot):
    nx, ny, nz = dims
    n = nx * 2 * ny * nz
    h, nb = panel_inverse.shape[3], panel_inverse.shape[4]
    angles = first_rhs.shape[3]
    count = trail_factor.shape[3]
    kind = BF16 if h % 16 == 0 else F32
    lanes = -(-4 * h // 128) * 128
    below = panel_below.reshape(2, 2, h, n, h).transpose(3, 2, 0, 1, 4).reshape(n, h, 4 * h)
    below = jnp.pad(below.astype(kind), ((0, 0), (0, 0), (0, lanes - 4 * h)))
    widest = max(nx, ny, nz, nx + ny)
    vmem = pl.BlockSpec(memory_space=pltpu.VMEM)
    hbm = pl.BlockSpec(memory_space=pl.ANY)
    panel_solution, trail_update = pl.pallas_call(
        functools.partial(kernel, dims),
        out_shape=(
            jax.ShapeDtypeStruct((2, 2, 2, h, angles), BF16),
            jax.ShapeDtypeStruct(trail_rhs.shape, BF16),
        ),
        in_specs=[vmem, vmem, vmem, hbm, hbm, hbm],
        out_specs=(vmem, hbm),
        scratch_shapes=[
            pltpu.VMEM(first_rhs.shape, BF16),
            pltpu.VMEM(trail_factor.shape, BF16),
            pltpu.VMEM(trail_rhs.shape, BF16),
            pltpu.VMEM(trail_rhs.shape, F32),
            pltpu.VMEM((12, nx, 2, nz, ny, h, angles), kind),
            pltpu.VMEM((n, h, lanes), kind),
            pltpu.SemaphoreType.DMA((2,)),
            pltpu.SemaphoreType.DMA((2, 2)),
            pltpu.SemaphoreType.DMA((2,)),
            pltpu.SemaphoreType.DMA((2,)),
            pltpu.SemaphoreType.DMA((2, 4, 12, widest)),
            pltpu.SemaphoreType.DMA((n,)),
            pltpu.SemaphoreType.DMA((n,)),
        ],
        compiler_params=pltpu.CompilerParams(
            collective_id=0, has_side_effects=True, vmem_limit_bytes=56 * 1024 * 1024
        ),
        cost_estimate=pl.CostEstimate(
            flops=32 * count * nb * angles, bytes_accessed=24 * 1024 * 1024, transcendentals=0
        ),
    )(panel_inverse, below, second_rhs, first_rhs, trail_factor, trail_rhs)
    partials = couple_partials(panel_solution, shape_tiles)
    dense_local = spread_vertices(partials, element_vertices, vertex_slot, vertex_slot.shape[0])
    vertex_gradient = lax.psum_scatter(dense_local, ("row", "col"), scatter_dimension=1, tiled=True)
    return (panel_solution, trail_update, vertex_gradient)


def solution(mesh):
    rows, cols = mesh.shape["row"], mesh.shape["col"]
    nx = max(rows // 2, 1)
    ny = nx if cols % nx == 0 else 1
    return jax.shard_map(
        functools.partial(body, (nx, ny, cols // ny)),
        mesh=mesh,
        in_specs=(
            P(None, None, None, ("row", "col"), None),
            P(None, None, ("row", "col"), None),
            P(None, None, None, ("row", "col"), None),
            P(),
            P(None, None, ("row", "col"), None),
            P(None, None, ("row", "col"), None),
            P(None, None, None, ("row", "col")),
            P(None, ("row", "col"), None),
            P(),
        ),
        out_specs=(
            P(None, None, None, ("row", "col"), None),
            P(None, None, ("row", "col"), None),
            P(None, ("row", "col")),
        ),
        check_vma=False,
    )
```

```python
import functools

import jax
import jax.numpy as jnp
from jax import lax
from jax.experimental import pallas as pl
from jax.experimental.pallas import tpu as pltpu
from jax.sharding import PartitionSpec as P

MESH = pl.DeviceIdType.MESH
F32 = jnp.float32
BF16 = jnp.bfloat16


def stack_rows(top, bottom):
    if top.shape[0] % 16:
        return jnp.concatenate([top.astype(F32), bottom.astype(F32)], axis=0).astype(BF16)
    return jnp.concatenate([top, bottom], axis=0)


def split_columns(parts, kind):
    h, width = parts[0].shape
    per, groups = 128 // h, width // 128
    wide = F32 if h % 16 else BF16
    rows = [jnp.concatenate([part[:, 128 * g:128 * (g + 1)] for part in parts], axis=1)
            for g in range(groups)]
    left = jnp.concatenate([row.astype(wide) for row in rows], axis=0).astype(BF16)
    source = lax.broadcasted_iota(jnp.int32, (512, per * 128), 0)
    target = lax.broadcasted_iota(jnp.int32, (512, per * 128), 1)
    lane = source % 128
    match = (lane // h == target // 128) & (target % 128 == (source // 128) * h + lane % h)
    moved = jnp.dot(left, jnp.where(match, 1.0, 0.0).astype(BF16), preferred_element_type=F32)
    return [moved[g * h:(g + 1) * h, r * 128:(r + 1) * 128].astype(kind)
            for g in range(groups) for r in range(per)]


def kernel(dims, inv, below_in, second, shapes, corners, slots, rhs_hbm, factor_hbm, trail_hbm,
           panel_out, update_hbm, vertex_out,
           rhs, factor, trail, update, held, columns, below, dense, sums,
           rhs_sem, factor_sem, trail_sem, update_sem,
           sems, column_send, column_recv, dense_send, dense_recv):
    nx, ny, nz = dims
    rows, cols = nx * 2, ny * nz
    n = rows * cols
    h = inv.shape[3]
    nb = inv.shape[4]
    angles = second.shape[3]
    steps = factor.shape[3] // trail_tile(factor.shape[3])
    tile = trail_tile(factor.shape[3])
    row, col = lax.axis_index("row"), lax.axis_index("col")
    x, core = row // 2, row % 2
    z, y = col // ny, col % ny
    me = row * cols + col
    sent = []

    loads = {}
    for s in range(2):
        loads["rhs", s] = pltpu.make_async_copy(rhs_hbm.at[s], rhs.at[s], rhs_sem.at[s])
        loads["rhs", s].start()

    barrier = pltpu.get_barrier_semaphore()

    def greet(k, carry):
        other = lax.rem(me + k, n)
        pl.semaphore_signal(barrier, inc=1, device_id=(other // cols, other % cols),
                            device_id_type=MESH)
        return carry

    lax.fori_loop(1, n, greet, 0)
    for t in range(2):
        for s in range(2):
            loads["factor", s, t] = pltpu.make_async_copy(
                factor_hbm.at[s, t], factor.at[s, t], factor_sem.at[s, t])
            loads["factor", s, t].start()
            if t == 0:
                loads["trail", s] = pltpu.make_async_copy(
                    trail_hbm.at[s], trail.at[s], trail_sem.at[s])
                loads["trail", s].start()

    def column_copy(target, source):
        return pltpu.make_async_remote_copy(
            src_ref=below.at[target], dst_ref=columns.at[source],
            send_sem=column_send.at[target], recv_sem=column_recv.at[source],
            device_id=(target // cols, target % cols), device_id_type=MESH)

    def remote(index, stage, k, region, target):
        copy = pltpu.make_async_remote_copy(
            src_ref=held.at[(index,) + region], dst_ref=held.at[(index,) + region],
            send_sem=sems.at[0, stage, index, k], recv_sem=sems.at[1, stage, index, k],
            device_id=target, device_id_type=MESH)
        return copy

    def send(index, stage, k, region, target):
        copy = remote(index, stage, k, region, target)
        copy.start()
        sent.append(copy)

    def receive(index, stage, k, region):
        remote(index, stage, k, region, (row, col)).wait_recv()

    every = slice(None)

    def spread(round_, s, make_block):
        indices = [(round_ * 2 + s) * 2 + p for p in range(2)]
        mate = (x * 2 + 1 - core, col)
        real, imag = make_block()
        for i, part in zip(indices, (real, imag)):
            held[i, x, core, z, y] = part.astype(held.dtype)
            for k in range(1, nz):
                send(i, 0, k, (x, core, z, y), (row, lax.rem(z + k, nz) * ny + y))
        yield
        for p, i in enumerate(indices):
            for k in range(1, nz):
                receive(i, 0, k, (x, core, lax.rem(z + nz - k, nz), y))
            line = (x, core, every, y)
            if p == 0:
                for k in range(1, ny):
                    send(i, 1, k, line, (row, z * ny + lax.rem(y + k, ny)))
            else:
                for k in range(1, nx):
                    send(i, 1, k, line, (lax.rem(x + k, nx) * 2 + core, col))
            send(i, 3, 0, line, mate)
        yield
        for p, i in enumerate(indices):
            if p == 0:
                got = [(x, core, every, lax.rem(y + ny - k, ny)) for k in range(1, ny)]
            else:
                got = [(lax.rem(x + nx - k, nx), core, every, y) for k in range(1, nx)]
            for k, region in enumerate(got):
                receive(i, 1, k + 1, region)
            if p == 0:
                for k in range(1, nx):
                    send(i, 2, k, (x, core), (lax.rem(x + k, nx) * 2 + core, col))
            else:
                for k in range(1, ny):
                    send(i, 2, k, (every, core, every, y), (row, z * ny + lax.rem(y + k, ny)))
            for k, region in enumerate(got):
                send(i, 3, 1 + k, region, mate)
        yield
        for p, i in enumerate(indices):
            if p == 0:
                got = [(lax.rem(x + nx - k, nx), core) for k in range(1, nx)]
            else:
                got = [(every, core, every, lax.rem(y + ny - k, ny)) for k in range(1, ny)]
            for k, region in enumerate(got):
                receive(i, 2, k + 1, region)
                base = ny if p == 0 else nx
                send(i, 3, base + k, region, mate)
        yield
        far = 1 - core
        for p, i in enumerate(indices):
            receive(i, 3, 0, (x, far, every, y))
            if p == 0:
                got = [(x, far, every, lax.rem(y + ny - k, ny)) for k in range(1, ny)]
                got += [(lax.rem(x + nx - k, nx), far) for k in range(1, nx)]
            else:
                got = [(lax.rem(x + nx - k, nx), far, every, y) for k in range(1, nx)]
                got += [(every, far, every, lax.rem(y + ny - k, ny)) for k in range(1, ny)]
            for k, region in enumerate(got):
                receive(i, 3, 1 + k, region)

    def gathered(round_, s, p):
        block = held[(round_ * 2 + s) * 2 + p]
        return block.reshape(nb, angles).astype(BF16)

    def dot(a, b):
        return jnp.dot(a, b, preferred_element_type=F32)

    def solve(s, panel, right):
        left = stack_rows(inv[s, panel, 0], inv[s, panel, 1])
        by_real, by_imag = dot(left, right[0]), dot(left, right[1])
        real = (by_real[:h] - by_imag[h:]).astype(BF16)
        imag = (by_imag[:h] + by_real[h:]).astype(BF16)
        panel_out[s, panel, 0] = real
        panel_out[s, panel, 1] = imag
        return real, imag

    def first_block(s):
        loads["rhs", s].wait()
        return solve(s, 0, (rhs[s, 0], rhs[s, 1]))

    def right_block(s):
        left = columns[...].astype(BF16).reshape(nb, columns.shape[2])
        products = [lax.dot_general(left, gathered(0, s, p), (((0,), (0,)), ((), ())),
                                    preferred_element_type=F32) for p in range(2)]
        a, b = 2 * s * h, (2 * s + 1) * h
        real = products[0][a:a + h] - products[1][b:b + h]
        imag = products[1][a:a + h] + products[0][b:b + h]
        return (second[s, 0].astype(F32) - real).astype(BF16), (
            second[s, 1].astype(F32) - imag).astype(BF16)

    def second_block(s):
        return solve(s, 1, (gathered(1, s, 0), gathered(1, s, 1)))

    def trail_part(s, t, part):
        at = pl.ds(part * tile, tile)
        solved = [gathered(2 * t, s, p) for p in range(2)]
        fr, fi = factor[s, t, 0, at, :], factor[s, t, 1, at, :]
        real = dot(fr, solved[0]) - dot(fi, solved[1])
        imag = dot(fr, solved[1]) + dot(fi, solved[0])
        if t == 0:
            update[s, 0, at, :] = trail[s, 0, at, :].astype(F32) - real
            update[s, 1, at, :] = trail[s, 1, at, :].astype(F32) - imag
        else:
            trail[s, 0, at, :] = (update[s, 0, at, :] - real).astype(BF16)
            trail[s, 1, at, :] = (update[s, 1, at, :] - imag).astype(BF16)

    def trail_run(s, t, first, last):
        if first == 0:
            loads["factor", s, t].wait()
            if t == 0:
                loads["trail", s].wait()
        for part in range(first, last):
            trail_part(s, t, part)

    def chain(s):
        yield from spread(0, s, lambda: first_block(s))
        yield from spread(1, s, lambda: right_block(s))
        yield from spread(2, s, lambda: second_block(s))

    def vertex_copy(target, source):
        return pltpu.make_async_remote_copy(
            src_ref=dense.at[target], dst_ref=sums.at[source],
            send_sem=dense_send.at[target], recv_sem=dense_recv.at[source],
            device_id=(target // cols, target % cols), device_id_type=MESH)

    def vertex_partials(t):
        fr, fi = panel_out[0, t, 0].astype(F32), panel_out[0, t, 1].astype(F32)
        ar, ai = panel_out[1, t, 0].astype(F32), panel_out[1, t, 1].astype(F32)
        ones = jnp.ones((8, angles), F32)

        def over_angles(values):
            return lax.dot_general(ones, values, (((1,), (1,)), ((), ())),
                                   precision=lax.Precision.HIGHEST,
                                   preferred_element_type=F32)[:1]

        real, imag = over_angles(fr * ar - fi * ai), over_angles(fr * ai + fi * ar)
        place = lax.broadcasted_iota(jnp.int32, (h, slots.shape[1]), 1)
        total = None
        for c in range(3):
            named = corners[t, :, c:c + 1] == place
            slot = jnp.sum(jnp.where(named, slots[...], 0), axis=1, keepdims=True)
            hot = jnp.where(slot == place, 1.0, 0.0).astype(F32)
            at = pl.ds(3 * c, 3)
            values = shapes[1, at, t, :] * imag - shapes[0, at, t, :] * real
            term = jnp.dot(values, hot, precision=lax.Precision.HIGHEST,
                           preferred_element_type=F32)
            total = term if total is None else total + term
        return total

    def vertex_send():
        total = vertex_partials(0) + vertex_partials(1)
        count = total.shape[1]
        flat = jnp.concatenate([total, jnp.zeros((125, count), F32)], axis=0)
        dense[...] = flat.T.reshape(dense.shape)
        sums[me] = dense[me]

        def start(k, carry):
            vertex_copy(lax.rem(me + k, n), me).start()
            return carry

        lax.fori_loop(1, n, start, 0)

    def vertex_collect():
        def wait(k, carry):
            vertex_copy(lax.rem(me + k, n), lax.rem(me + n - k, n)).wait()
            return carry

        lax.fori_loop(1, n, wait, 0)
        vertex_out[...] = jnp.sum(sums[...], axis=0).T[:3]

    pl.semaphore_wait(barrier, n - 1)

    chains = [chain(0), chain(1)]
    next(chains[0])
    next(chains[1])

    parts = [below_in[i, p] for i in range(2) for p in range(2)]
    for d, block in enumerate(split_columns(parts, below.dtype)):
        below[d] = block
    columns[me] = below[me]

    def scatter(k, carry):
        column_copy(lax.rem(me + k, n), me).start()
        return carry

    lax.fori_loop(1, n, scatter, 0)
    next(chains[0])
    next(chains[1])
    next(chains[0])
    next(chains[1])
    next(chains[0])

    def collect(k, carry):
        column_copy(lax.rem(me + k, n), lax.rem(me + n - k, n)).wait()
        return carry

    lax.fori_loop(1, n, collect, 0)
    half = steps // 2
    next(chains[0])
    next(chains[1])
    next(chains[0])
    next(chains[1])
    trail_run(0, 0, 0, half)
    next(chains[0])
    next(chains[1])
    trail_run(0, 0, half, steps)
    next(chains[0])
    next(chains[1])
    next(chains[0])
    next(chains[1])
    next(chains[0])
    next(chains[1])
    vertex_send()
    trail_run(1, 0, 0, half)
    next(chains[0])
    next(chains[1])
    trail_run(1, 0, half, steps)
    next(chains[0])
    next(chains[1])
    next(chains[0], None)
    next(chains[1])
    stores = []
    trail_run(0, 1, 0, steps)
    stores.append(pltpu.make_async_copy(trail.at[0], update_hbm.at[0], update_sem.at[0]))
    stores[0].start()
    next(chains[1], None)
    trail_run(1, 1, 0, steps)
    stores.append(pltpu.make_async_copy(trail.at[1], update_hbm.at[1], update_sem.at[1]))
    stores[1].start()
    vertex_collect()
    for copy in sent:
        copy.wait_send()
    for copy in stores:
        copy.wait()


def trail_tile(count):
    return min(count, 256)


def body(dims, panel_inverse, panel_below, trail_factor, first_rhs, second_rhs, trail_rhs,
         shape_tiles, element_vertices, vertex_slot):
    nx, ny, nz = dims
    n = nx * 2 * ny * nz
    h, nb = panel_inverse.shape[3], panel_inverse.shape[4]
    angles = first_rhs.shape[3]
    count = trail_factor.shape[3]
    kind = BF16 if h % 16 == 0 else F32
    lanes = 128
    slot_count = vertex_slot.shape[0]
    widest = max(nx, ny, nz, nx + ny)
    vmem = pl.BlockSpec(memory_space=pltpu.VMEM)
    hbm = pl.BlockSpec(memory_space=pl.ANY)
    return pl.pallas_call(
        functools.partial(kernel, dims),
        out_shape=(
            jax.ShapeDtypeStruct((2, 2, 2, h, angles), BF16),
            jax.ShapeDtypeStruct(trail_rhs.shape, BF16),
            jax.ShapeDtypeStruct((3, slot_count // n), F32),
        ),
        in_specs=[vmem] * 6 + [hbm] * 3,
        out_specs=(vmem, hbm, vmem),
        scratch_shapes=[
            pltpu.VMEM(first_rhs.shape, BF16),
            pltpu.VMEM(trail_factor.shape, BF16),
            pltpu.VMEM(trail_rhs.shape, BF16),
            pltpu.VMEM(trail_rhs.shape, F32),
            pltpu.VMEM((12, nx, 2, nz, ny, h, angles), kind),
            pltpu.VMEM((n, h, lanes), kind),
            pltpu.VMEM((n, h, lanes), kind),
            pltpu.VMEM((n, slot_count // n, 128), F32),
            pltpu.VMEM((n, slot_count // n, 128), F32),
            pltpu.SemaphoreType.DMA((2,)),
            pltpu.SemaphoreType.DMA((2, 2)),
            pltpu.SemaphoreType.DMA((2,)),
            pltpu.SemaphoreType.DMA((2,)),
            pltpu.SemaphoreType.DMA((2, 4, 12, widest)),
            pltpu.SemaphoreType.DMA((n,)),
            pltpu.SemaphoreType.DMA((n,)),
            pltpu.SemaphoreType.DMA((n,)),
            pltpu.SemaphoreType.DMA((n,)),
        ],
        compiler_params=pltpu.CompilerParams(
            collective_id=0, has_side_effects=True, vmem_limit_bytes=56 * 1024 * 1024
        ),
        cost_estimate=pl.CostEstimate(
            flops=32 * count * nb * angles, bytes_accessed=24 * 1024 * 1024, transcendentals=0
        ),
    )(panel_inverse, panel_below, second_rhs, shape_tiles, element_vertices,
      vertex_slot.reshape(1, slot_count), first_rhs, trail_factor, trail_rhs)


def solution(mesh):
    rows, cols = mesh.shape["row"], mesh.shape["col"]
    nx = max(rows // 2, 1)
    ny = nx if cols % nx == 0 else 1
    return jax.shard_map(
        functools.partial(body, (nx, ny, cols // ny)),
        mesh=mesh,
        in_specs=(
            P(None, None, None, ("row", "col"), None),
            P(None, None, ("row", "col"), None),
            P(None, None, None, ("row", "col"), None),
            P(),
            P(None, None, ("row", "col"), None),
            P(None, None, ("row", "col"), None),
            P(None, None, None, ("row", "col")),
            P(None, ("row", "col"), None),
            P(),
        ),
        out_specs=(
            P(None, None, None, ("row", "col"), None),
            P(None, None, ("row", "col"), None),
            P(None, ("row", "col")),
        ),
        check_vma=False,
    )
```

```python
import functools

import jax
import jax.numpy as jnp
from jax import lax
from jax.experimental import pallas as pl
from jax.experimental.pallas import tpu as pltpu
from jax.sharding import PartitionSpec as P

MESH = pl.DeviceIdType.MESH
F32 = jnp.float32
BF16 = jnp.bfloat16


def stack_rows(top, bottom):
    if top.shape[0] % 16:
        return jnp.concatenate([top.astype(F32), bottom.astype(F32)], axis=0).astype(BF16)
    return jnp.concatenate([top, bottom], axis=0)


def split_columns(parts, kind):
    h, width = parts[0].shape
    per, groups = 128 // h, width // 128
    wide = F32 if h % 16 else BF16
    rows = [jnp.concatenate([part[:, 128 * g:128 * (g + 1)] for part in parts], axis=1)
            for g in range(groups)]
    left = jnp.concatenate([row.astype(wide) for row in rows], axis=0).astype(BF16)
    source = lax.broadcasted_iota(jnp.int32, (512, per * 128), 0)
    target = lax.broadcasted_iota(jnp.int32, (512, per * 128), 1)
    lane = source % 128
    match = (lane // h == target // 128) & (target % 128 == (source // 128) * h + lane % h)
    moved = jnp.dot(left, jnp.where(match, 1.0, 0.0).astype(BF16), preferred_element_type=F32)
    return [moved[g * h:(g + 1) * h, r * 128:(r + 1) * 128].astype(kind)
            for g in range(groups) for r in range(per)]


def kernel(dims, inv, below_in, second, shapes, corners, slots, rhs_hbm, factor_hbm, trail_hbm,
           panel_out, update_hbm, vertex_out,
           rhs, factor, trail, update, held, columns, turned, below, dense, sums,
           rhs_sem, factor_sem, trail_sem, update_sem,
           sems, column_send, column_recv, dense_send, dense_recv):
    nx, ny, nz = dims
    rows, cols = nx * 2, ny * nz
    n = rows * cols
    h = inv.shape[3]
    nb = inv.shape[4]
    angles = second.shape[3]
    steps = factor.shape[3] // trail_tile(factor.shape[3])
    tile = trail_tile(factor.shape[3])
    row, col = lax.axis_index("row"), lax.axis_index("col")
    x, core = row // 2, row % 2
    z, y = col // ny, col % ny
    me = row * cols + col
    sent = []

    loads = {}
    for s in range(2):
        loads["rhs", s] = pltpu.make_async_copy(rhs_hbm.at[s], rhs.at[s], rhs_sem.at[s])
        loads["rhs", s].start()

    barrier = pltpu.get_barrier_semaphore()

    def greet(k, carry):
        other = lax.rem(me + k, n)
        pl.semaphore_signal(barrier, inc=1, device_id=(other // cols, other % cols),
                            device_id_type=MESH)
        return carry

    lax.fori_loop(1, n, greet, 0)
    for t in range(2):
        for s in range(2):
            loads["factor", s, t] = pltpu.make_async_copy(
                factor_hbm.at[s, t], factor.at[s, t], factor_sem.at[s, t])
            loads["factor", s, t].start()
            if t == 0:
                loads["trail", s] = pltpu.make_async_copy(
                    trail_hbm.at[s], trail.at[s], trail_sem.at[s])
                loads["trail", s].start()

    def column_copy(target, source):
        return pltpu.make_async_remote_copy(
            src_ref=below.at[target], dst_ref=columns.at[source],
            send_sem=column_send.at[target], recv_sem=column_recv.at[source],
            device_id=(target // cols, target % cols), device_id_type=MESH)

    def remote(index, stage, k, region, target):
        copy = pltpu.make_async_remote_copy(
            src_ref=held.at[(index,) + region], dst_ref=held.at[(index,) + region],
            send_sem=sems.at[0, stage, index, k], recv_sem=sems.at[1, stage, index, k],
            device_id=target, device_id_type=MESH)
        return copy

    def send(index, stage, k, region, target):
        copy = remote(index, stage, k, region, target)
        copy.start()
        sent.append(copy)

    def receive(index, stage, k, region):
        remote(index, stage, k, region, (row, col)).wait_recv()

    every = slice(None)

    def spread(round_, s, make_block):
        indices = [(round_ * 2 + s) * 2 + p for p in range(2)]
        mate = (x * 2 + 1 - core, col)
        real, imag = make_block()
        for i, part in zip(indices, (real, imag)):
            held[i, x, core, z, y] = part.astype(held.dtype)
            for k in range(1, nz):
                send(i, 0, k, (x, core, z, y), (row, lax.rem(z + k, nz) * ny + y))
        yield
        for p, i in enumerate(indices):
            for k in range(1, nz):
                receive(i, 0, k, (x, core, lax.rem(z + nz - k, nz), y))
            line = (x, core, every, y)
            if p == 0:
                for k in range(1, ny):
                    send(i, 1, k, line, (row, z * ny + lax.rem(y + k, ny)))
            else:
                for k in range(1, nx):
                    send(i, 1, k, line, (lax.rem(x + k, nx) * 2 + core, col))
            send(i, 3, 0, line, mate)
        yield
        for p, i in enumerate(indices):
            if p == 0:
                got = [(x, core, every, lax.rem(y + ny - k, ny)) for k in range(1, ny)]
            else:
                got = [(lax.rem(x + nx - k, nx), core, every, y) for k in range(1, nx)]
            for k, region in enumerate(got):
                receive(i, 1, k + 1, region)
            if p == 0:
                for k in range(1, nx):
                    send(i, 2, k, (x, core), (lax.rem(x + k, nx) * 2 + core, col))
            else:
                for k in range(1, ny):
                    send(i, 2, k, (every, core, every, y), (row, z * ny + lax.rem(y + k, ny)))
            for k, region in enumerate(got):
                send(i, 3, 1 + k, region, mate)
        yield
        for p, i in enumerate(indices):
            if p == 0:
                got = [(lax.rem(x + nx - k, nx), core) for k in range(1, nx)]
            else:
                got = [(every, core, every, lax.rem(y + ny - k, ny)) for k in range(1, ny)]
            for k, region in enumerate(got):
                receive(i, 2, k + 1, region)
                base = ny if p == 0 else nx
                send(i, 3, base + k, region, mate)
        yield
        far = 1 - core
        for p, i in enumerate(indices):
            receive(i, 3, 0, (x, far, every, y))
            if p == 0:
                got = [(x, far, every, lax.rem(y + ny - k, ny)) for k in range(1, ny)]
                got += [(lax.rem(x + nx - k, nx), far) for k in range(1, nx)]
            else:
                got = [(lax.rem(x + nx - k, nx), far, every, y) for k in range(1, nx)]
                got += [(every, far, every, lax.rem(y + ny - k, ny)) for k in range(1, ny)]
            for k, region in enumerate(got):
                receive(i, 3, 1 + k, region)

    def gathered(round_, s, p):
        block = held[(round_ * 2 + s) * 2 + p]
        return block.reshape(nb, angles).astype(BF16)

    def dot(a, b):
        return jnp.dot(a, b, preferred_element_type=F32)

    def solve(s, panel, right):
        left = stack_rows(inv[s, panel, 0], inv[s, panel, 1])
        by_real, by_imag = dot(left, right[0]), dot(left, right[1])
        real = (by_real[:h] - by_imag[h:]).astype(BF16)
        imag = (by_imag[:h] + by_real[h:]).astype(BF16)
        panel_out[s, panel, 0] = real
        panel_out[s, panel, 1] = imag
        return real, imag

    def first_block(s):
        loads["rhs", s].wait()
        return solve(s, 0, (rhs[s, 0], rhs[s, 1]))

    def right_block(s):
        left = turned[2 * s * h:2 * (s + 1) * h]
        products = [dot(left, gathered(0, s, p)) for p in range(2)]
        real = products[0][:h] - products[1][h:]
        imag = products[1][:h] + products[0][h:]
        return (second[s, 0].astype(F32) - real).astype(BF16), (
            second[s, 1].astype(F32) - imag).astype(BF16)

    def second_block(s):
        return solve(s, 1, (gathered(1, s, 0), gathered(1, s, 1)))

    def trail_part(s, t, part):
        at = pl.ds(part * tile, tile)
        solved = [gathered(2 * t, s, p) for p in range(2)]
        fr, fi = factor[s, t, 0, at, :], factor[s, t, 1, at, :]
        real = dot(fr, solved[0]) - dot(fi, solved[1])
        imag = dot(fr, solved[1]) + dot(fi, solved[0])
        if t == 0:
            update[s, 0, at, :] = trail[s, 0, at, :].astype(F32) - real
            update[s, 1, at, :] = trail[s, 1, at, :].astype(F32) - imag
        else:
            trail[s, 0, at, :] = (update[s, 0, at, :] - real).astype(BF16)
            trail[s, 1, at, :] = (update[s, 1, at, :] - imag).astype(BF16)

    def trail_run(s, t, first, last):
        if first == 0:
            loads["factor", s, t].wait()
            if t == 0:
                loads["trail", s].wait()
        for part in range(first, last):
            trail_part(s, t, part)

    def chain(s):
        yield from spread(0, s, lambda: firsts[s])
        yield from spread(1, s, lambda: right_block(s))
        yield from spread(2, s, lambda: second_block(s))

    def vertex_copy(target, source):
        return pltpu.make_async_remote_copy(
            src_ref=dense.at[target], dst_ref=sums.at[source],
            send_sem=dense_send.at[target], recv_sem=dense_recv.at[source],
            device_id=(target // cols, target % cols), device_id_type=MESH)

    def vertex_partials(t):
        fr, fi = panel_out[0, t, 0].astype(F32), panel_out[0, t, 1].astype(F32)
        ar, ai = panel_out[1, t, 0].astype(F32), panel_out[1, t, 1].astype(F32)
        ones = jnp.ones((8, angles), F32)

        def over_angles(values):
            return lax.dot_general(ones, values, (((1,), (1,)), ((), ())),
                                   precision=lax.Precision.HIGHEST,
                                   preferred_element_type=F32)[:1]

        real, imag = over_angles(fr * ar - fi * ai), over_angles(fr * ai + fi * ar)
        count = slots.shape[1]
        place = lax.broadcasted_iota(jnp.int32, (count, h), 0)
        owner = jnp.broadcast_to(slots[...].astype(F32), (8, count)).T[:, :1]
        total = None
        for c in range(3):
            named = corners[c, t:t + 1, :] == place
            slot = jnp.sum(jnp.where(named, owner, 0.0), axis=0, keepdims=True)
            hot = jnp.where(slot == place.astype(F32), 1.0, 0.0)
            at = pl.ds(3 * c, 3)
            values = shapes[1, at, t, :] * imag - shapes[0, at, t, :] * real
            values = jnp.concatenate([values, jnp.zeros((125, h), F32)], axis=0)
            term = lax.dot_general(hot, values, (((1,), (1,)), ((), ())),
                                   precision=lax.Precision.HIGHEST,
                                   preferred_element_type=F32)
            total = term if total is None else total + term
        return total

    def vertex_send():
        total = vertex_partials(0) + vertex_partials(1)
        dense[...] = total.reshape(dense.shape)
        sums[me] = dense[me]

        def start(k, carry):
            vertex_copy(lax.rem(me + k, n), me).start()
            return carry

        lax.fori_loop(1, n, start, 0)

    def vertex_collect():
        def wait(k, carry):
            vertex_copy(lax.rem(me + k, n), lax.rem(me + n - k, n)).wait()
            return carry

        lax.fori_loop(1, n, wait, 0)
        vertex_out[...] = jnp.sum(sums[...], axis=0).T[:3]

    firsts = [first_block(s) for s in range(2)]
    pl.semaphore_wait(barrier, n - 1)

    chains = [chain(0), chain(1)]
    next(chains[0])
    next(chains[1])

    parts = [below_in[i, p] for i in range(2) for p in range(2)]
    for d, block in enumerate(split_columns(parts, below.dtype)):
        below[d] = block
    columns[me] = below[me]

    def scatter(k, carry):
        column_copy(lax.rem(me + k, n), me).start()
        return carry

    lax.fori_loop(1, n, scatter, 0)
    next(chains[0])
    next(chains[1])
    next(chains[0])
    next(chains[1])
    next(chains[0])

    def collect(k, carry):
        column_copy(lax.rem(me + k, n), lax.rem(me + n - k, n)).wait()
        return carry

    lax.fori_loop(1, n, collect, 0)
    turned[...] = columns[...].astype(F32).reshape(nb, columns.shape[2]).T.astype(BF16)
    half = steps // 2
    next(chains[0])
    next(chains[1])
    next(chains[0])
    next(chains[1])
    trail_run(0, 0, 0, half)
    next(chains[0])
    next(chains[1])
    trail_run(0, 0, half, steps)
    next(chains[0])
    next(chains[1])
    next(chains[0])
    next(chains[1])
    next(chains[0])
    next(chains[1])
    trail_run(1, 0, 0, half)
    next(chains[0])
    next(chains[1])
    trail_run(1, 0, half, steps)
    next(chains[0])
    next(chains[1])
    next(chains[0], None)
    next(chains[1])
    stores = []
    vertex_send()
    trail_run(0, 1, 0, steps)
    stores.append(pltpu.make_async_copy(trail.at[0], update_hbm.at[0], update_sem.at[0]))
    stores[0].start()
    next(chains[1], None)
    trail_run(1, 1, 0, steps)
    stores.append(pltpu.make_async_copy(trail.at[1], update_hbm.at[1], update_sem.at[1]))
    stores[1].start()
    vertex_collect()
    for copy in sent:
        copy.wait_send()
    for copy in stores:
        copy.wait()


def trail_tile(count):
    return min(count, 256)


def body(dims, panel_inverse, panel_below, trail_factor, first_rhs, second_rhs, trail_rhs,
         shape_tiles, element_vertices, vertex_slot):
    nx, ny, nz = dims
    n = nx * 2 * ny * nz
    h, nb = panel_inverse.shape[3], panel_inverse.shape[4]
    angles = first_rhs.shape[3]
    count = trail_factor.shape[3]
    kind = BF16 if h % 16 == 0 else F32
    lanes = 128
    slot_count = vertex_slot.shape[0]
    widest = max(nx, ny, nz, nx + ny)
    vmem = pl.BlockSpec(memory_space=pltpu.VMEM)
    hbm = pl.BlockSpec(memory_space=pl.ANY)
    return pl.pallas_call(
        functools.partial(kernel, dims),
        out_shape=(
            jax.ShapeDtypeStruct((2, 2, 2, h, angles), BF16),
            jax.ShapeDtypeStruct(trail_rhs.shape, BF16),
            jax.ShapeDtypeStruct((3, slot_count // n), F32),
        ),
        in_specs=[vmem] * 6 + [pl.BlockSpec(memory_space=pltpu.HBM)] * 3,
        out_specs=(vmem, hbm, vmem),
        scratch_shapes=[
            pltpu.VMEM(first_rhs.shape, BF16),
            pltpu.VMEM(trail_factor.shape, BF16),
            pltpu.VMEM(trail_rhs.shape, BF16),
            pltpu.VMEM(trail_rhs.shape, F32),
            pltpu.VMEM((12, nx, 2, nz, ny, h, angles), kind),
            pltpu.VMEM((n, h, lanes), kind),
            pltpu.VMEM((lanes, nb), BF16),
            pltpu.VMEM((n, h, lanes), kind),
            pltpu.VMEM((n, slot_count // n, 128), F32),
            pltpu.VMEM((n, slot_count // n, 128), F32),
            pltpu.SemaphoreType.DMA((2,)),
            pltpu.SemaphoreType.DMA((2, 2)),
            pltpu.SemaphoreType.DMA((2,)),
            pltpu.SemaphoreType.DMA((2,)),
            pltpu.SemaphoreType.DMA((2, 4, 12, widest)),
            pltpu.SemaphoreType.DMA((n,)),
            pltpu.SemaphoreType.DMA((n,)),
            pltpu.SemaphoreType.DMA((n,)),
            pltpu.SemaphoreType.DMA((n,)),
        ],
        compiler_params=pltpu.CompilerParams(
            collective_id=0, has_side_effects=True, vmem_limit_bytes=40 * 1024 * 1024
        ),
        cost_estimate=pl.CostEstimate(
            flops=32 * count * nb * angles, bytes_accessed=24 * 1024 * 1024, transcendentals=0
        ),
    )(panel_inverse, panel_below, second_rhs, shape_tiles, element_vertices.transpose(2, 0, 1),
      vertex_slot.reshape(1, slot_count), first_rhs, trail_factor, trail_rhs)


def solution(mesh):
    rows, cols = mesh.shape["row"], mesh.shape["col"]
    nx = max(rows // 2, 1)
    ny = nx if cols % nx == 0 else 1
    return jax.shard_map(
        functools.partial(body, (nx, ny, cols // ny)),
        mesh=mesh,
        in_specs=(
            P(None, None, None, ("row", "col"), None),
            P(None, None, ("row", "col"), None),
            P(None, None, None, ("row", "col"), None),
            P(),
            P(None, None, ("row", "col"), None),
            P(None, None, ("row", "col"), None),
            P(None, None, None, ("row", "col")),
            P(None, ("row", "col"), None),
            P(),
        ),
        out_specs=(
            P(None, None, None, ("row", "col"), None),
            P(None, None, ("row", "col"), None),
            P(None, ("row", "col")),
        ),
        check_vma=False,
    )
```

```python
import functools

import jax
import jax.numpy as jnp
from jax import lax
from jax.experimental import pallas as pl
from jax.experimental.pallas import tpu as pltpu
from jax.sharding import PartitionSpec as P

MESH = pl.DeviceIdType.MESH
F32 = jnp.float32
BF16 = jnp.bfloat16


def stack_rows(top, bottom):
    if top.shape[0] % 16:
        return jnp.concatenate([top.astype(F32), bottom.astype(F32)], axis=0).astype(BF16)
    return jnp.concatenate([top, bottom], axis=0)


def split_columns(parts, kind):
    h, width = parts[0].shape
    per, groups = 128 // h, width // 128
    wide = F32 if h % 16 else BF16
    rows = [jnp.concatenate([part[:, 128 * g:128 * (g + 1)] for part in parts], axis=1)
            for g in range(groups)]
    left = jnp.concatenate([row.astype(wide) for row in rows], axis=0).astype(BF16)
    source = lax.broadcasted_iota(jnp.int32, (512, per * 128), 0)
    target = lax.broadcasted_iota(jnp.int32, (512, per * 128), 1)
    lane = source % 128
    match = (lane // h == target // 128) & (target % 128 == (source // 128) * h + lane % h)
    moved = jnp.dot(left, jnp.where(match, 1.0, 0.0).astype(BF16), preferred_element_type=F32)
    return [moved[g * h:(g + 1) * h, r * 128:(r + 1) * 128].astype(kind)
            for g in range(groups) for r in range(per)]


def kernel(dims, inv, below_in, second, shapes, corners, slots, rhs_hbm, factor_hbm, trail_hbm,
           panel_out, update_hbm, vertex_out,
           rhs, factor, trail, update, held, columns, turned, below, dense, sums,
           rhs_sem, factor_sem, trail_sem, update_sem,
           sems, column_send, column_recv, dense_send, dense_recv):
    nx, ny, nz = dims
    rows, cols = nx * 2, ny * nz
    n = rows * cols
    h = inv.shape[3]
    nb = inv.shape[4]
    angles = second.shape[3]
    steps = factor.shape[3] // trail_tile(factor.shape[3])
    tile = trail_tile(factor.shape[3])
    row, col = lax.axis_index("row"), lax.axis_index("col")
    x, core = row // 2, row % 2
    z, y = col // ny, col % ny
    me = row * cols + col
    sent = []

    loads = {}
    for s in range(2):
        loads["rhs", s] = pltpu.make_async_copy(rhs_hbm.at[s], rhs.at[s], rhs_sem.at[s])
        loads["rhs", s].start()

    barrier = pltpu.get_barrier_semaphore()

    def greet(k, carry):
        other = lax.rem(me + k, n)
        pl.semaphore_signal(barrier, inc=1, device_id=(other // cols, other % cols),
                            device_id_type=MESH)
        return carry

    lax.fori_loop(1, n, greet, 0)
    for t in range(2):
        for s in range(2):
            loads["factor", s, t] = pltpu.make_async_copy(
                factor_hbm.at[s, t], factor.at[s, t], factor_sem.at[s, t])
            loads["factor", s, t].start()
            if t == 0:
                loads["trail", s] = pltpu.make_async_copy(
                    trail_hbm.at[s], trail.at[s], trail_sem.at[s])
                loads["trail", s].start()

    def column_copy(target, source):
        return pltpu.make_async_remote_copy(
            src_ref=below.at[target], dst_ref=columns.at[source],
            send_sem=column_send.at[target], recv_sem=column_recv.at[source],
            device_id=(target // cols, target % cols), device_id_type=MESH)

    def remote(index, stage, k, region, target):
        copy = pltpu.make_async_remote_copy(
            src_ref=held.at[(index,) + region], dst_ref=held.at[(index,) + region],
            send_sem=sems.at[0, stage, index, k], recv_sem=sems.at[1, stage, index, k],
            device_id=target, device_id_type=MESH)
        return copy

    def send(index, stage, k, region, target):
        copy = remote(index, stage, k, region, target)
        copy.start()
        sent.append(copy)

    def receive(index, stage, k, region):
        remote(index, stage, k, region, (row, col)).wait_recv()

    every = slice(None)

    def spread(round_, s, make_block):
        indices = [(round_ * 2 + s) * 2 + p for p in range(2)]
        mate = (x * 2 + 1 - core, col)
        real, imag = make_block()
        for i, part in zip(indices, (real, imag)):
            held[i, x, core, z, y] = part.astype(held.dtype)
            for k in range(1, nz):
                send(i, 0, k, (x, core, z, y), (row, lax.rem(z + k, nz) * ny + y))
        yield
        for p, i in enumerate(indices):
            for k in range(1, nz):
                receive(i, 0, k, (x, core, lax.rem(z + nz - k, nz), y))
            line = (x, core, every, y)
            if p == 0:
                for k in range(1, ny):
                    send(i, 1, k, line, (row, z * ny + lax.rem(y + k, ny)))
            else:
                for k in range(1, nx):
                    send(i, 1, k, line, (lax.rem(x + k, nx) * 2 + core, col))
            send(i, 3, 0, line, mate)
        yield
        for p, i in enumerate(indices):
            if p == 0:
                got = [(x, core, every, lax.rem(y + ny - k, ny)) for k in range(1, ny)]
            else:
                got = [(lax.rem(x + nx - k, nx), core, every, y) for k in range(1, nx)]
            for k, region in enumerate(got):
                receive(i, 1, k + 1, region)
            if p == 0:
                for k in range(1, nx):
                    send(i, 2, k, (x, core), (lax.rem(x + k, nx) * 2 + core, col))
            else:
                for k in range(1, ny):
                    send(i, 2, k, (every, core, every, y), (row, z * ny + lax.rem(y + k, ny)))
            for k, region in enumerate(got):
                send(i, 3, 1 + k, region, mate)
        yield
        for p, i in enumerate(indices):
            if p == 0:
                got = [(lax.rem(x + nx - k, nx), core) for k in range(1, nx)]
            else:
                got = [(every, core, every, lax.rem(y + ny - k, ny)) for k in range(1, ny)]
            for k, region in enumerate(got):
                receive(i, 2, k + 1, region)
                base = ny if p == 0 else nx
                send(i, 3, base + k, region, mate)
        yield
        far = 1 - core
        for p, i in enumerate(indices):
            receive(i, 3, 0, (x, far, every, y))
            if p == 0:
                got = [(x, far, every, lax.rem(y + ny - k, ny)) for k in range(1, ny)]
                got += [(lax.rem(x + nx - k, nx), far) for k in range(1, nx)]
            else:
                got = [(lax.rem(x + nx - k, nx), far, every, y) for k in range(1, nx)]
                got += [(every, far, every, lax.rem(y + ny - k, ny)) for k in range(1, ny)]
            for k, region in enumerate(got):
                receive(i, 3, 1 + k, region)

    def gathered(round_, s, p):
        block = held[(round_ * 2 + s) * 2 + p]
        return block.reshape(nb, angles).astype(BF16)

    def dot(a, b):
        return jnp.dot(a, b, preferred_element_type=F32)

    def solve(s, panel, right):
        left = stack_rows(inv[s, panel, 0], inv[s, panel, 1])
        by_real, by_imag = dot(left, right[0]), dot(left, right[1])
        real = (by_real[:h] - by_imag[h:]).astype(BF16)
        imag = (by_imag[:h] + by_real[h:]).astype(BF16)
        panel_out[s, panel, 0] = real
        panel_out[s, panel, 1] = imag
        return real, imag

    def first_block(s):
        loads["rhs", s].wait()
        return solve(s, 0, (rhs[s, 0], rhs[s, 1]))

    def right_block(s):
        left = turned[2 * s * h:2 * (s + 1) * h]
        products = [dot(left, gathered(0, s, p)) for p in range(2)]
        real = products[0][:h] - products[1][h:]
        imag = products[1][:h] + products[0][h:]
        return (second[s, 0].astype(F32) - real).astype(BF16), (
            second[s, 1].astype(F32) - imag).astype(BF16)

    def second_block(s):
        return solve(s, 1, (gathered(1, s, 0), gathered(1, s, 1)))

    def trail_part(s, t, part):
        at = pl.ds(part * tile, tile)
        solved = [gathered(2 * t, s, p) for p in range(2)]
        fr, fi = factor[s, t, 0, at, :], factor[s, t, 1, at, :]
        real = dot(fr, solved[0]) - dot(fi, solved[1])
        imag = dot(fr, solved[1]) + dot(fi, solved[0])
        if t == 0:
            update[s, 0, at, :] = trail[s, 0, at, :].astype(F32) - real
            update[s, 1, at, :] = trail[s, 1, at, :].astype(F32) - imag
        else:
            trail[s, 0, at, :] = (update[s, 0, at, :] - real).astype(BF16)
            trail[s, 1, at, :] = (update[s, 1, at, :] - imag).astype(BF16)

    def trail_run(s, t, first, last):
        if first == 0:
            loads["factor", s, t].wait()
            if t == 0:
                loads["trail", s].wait()
        for part in range(first, last):
            trail_part(s, t, part)

    def chain(s):
        yield from spread(0, s, lambda: firsts[s])
        yield from spread(1, s, lambda: right_block(s))
        yield from spread(2, s, lambda: second_block(s))

    def vertex_copy(target, source):
        return pltpu.make_async_remote_copy(
            src_ref=dense.at[target], dst_ref=sums.at[source],
            send_sem=dense_send.at[target], recv_sem=dense_recv.at[source],
            device_id=(target // cols, target % cols), device_id_type=MESH)

    def vertex_partials(t):
        fr, fi = panel_out[0, t, 0].astype(F32), panel_out[0, t, 1].astype(F32)
        ar, ai = panel_out[1, t, 0].astype(F32), panel_out[1, t, 1].astype(F32)
        ones = jnp.ones((8, angles), F32)

        def over_angles(values):
            return lax.dot_general(ones, values, (((1,), (1,)), ((), ())),
                                   precision=lax.Precision.HIGHEST,
                                   preferred_element_type=F32)[:1]

        real, imag = over_angles(fr * ar - fi * ai), over_angles(fr * ai + fi * ar)
        count = slots.shape[1]
        place = lax.broadcasted_iota(jnp.int32, (count, h), 0)
        owner = jnp.broadcast_to(slots[...].astype(F32), (8, count)).T[:, :1]
        total = None
        for c in range(3):
            named = corners[c, t:t + 1, :] == place
            slot = jnp.sum(jnp.where(named, owner, 0.0), axis=0, keepdims=True)
            hot = jnp.where(slot == place.astype(F32), 1.0, 0.0)
            at = pl.ds(3 * c, 3)
            values = shapes[1, at, t, :] * imag - shapes[0, at, t, :] * real
            values = jnp.concatenate([values, jnp.zeros((125, h), F32)], axis=0)
            term = lax.dot_general(hot, values, (((1,), (1,)), ((), ())),
                                   precision=lax.Precision.HIGHEST,
                                   preferred_element_type=F32)
            total = term if total is None else total + term
        return total

    def vertex_send():
        total = vertex_partials(0) + vertex_partials(1)
        dense[...] = total.reshape(dense.shape)
        sums[me] = dense[me]

        def start(k, carry):
            vertex_copy(lax.rem(me + k, n), me).start()
            return carry

        lax.fori_loop(1, n, start, 0)

    def vertex_collect():
        def wait(k, carry):
            vertex_copy(lax.rem(me + k, n), lax.rem(me + n - k, n)).wait()
            return carry

        lax.fori_loop(1, n, wait, 0)
        vertex_out[...] = jnp.sum(sums[...], axis=0).T[:3]

    firsts = [first_block(s) for s in range(2)]
    pl.semaphore_wait(barrier, n - 1)

    chains = [chain(0), chain(1)]
    next(chains[0])
    parts = [below_in[i, p] for i in range(2) for p in range(2)]
    for d, block in enumerate(split_columns(parts, below.dtype)):
        below[d] = block
    columns[me] = below[me]

    def scatter(k, carry):
        column_copy(lax.rem(me + k, n), me).start()
        return carry

    lax.fori_loop(1, n, scatter, 0)
    next(chains[0])
    next(chains[1])
    next(chains[0])
    next(chains[0])
    next(chains[1])

    def collect(k, carry):
        column_copy(lax.rem(me + k, n), lax.rem(me + n - k, n)).wait()
        return carry

    lax.fori_loop(1, n, collect, 0)
    turned[...] = columns[...].astype(F32).reshape(nb, columns.shape[2]).T.astype(BF16)
    cuts = [steps * k // 4 for k in range(5)]
    for round_ in range(2):
        next(chains[0])
        next(chains[1])
        trail_run(round_, 0, cuts[0], cuts[1])
        next(chains[0])
        next(chains[1])
        trail_run(round_, 0, cuts[1], cuts[2])
        next(chains[0])
        next(chains[1])
        trail_run(round_, 0, cuts[2], cuts[3])
        next(chains[0])
        next(chains[1])
        if round_ == 1:
            vertex_send()
        trail_run(round_, 0, cuts[3], cuts[4])
    stores = []
    next(chains[0], None)
    next(chains[1])
    trail_run(0, 1, cuts[0], cuts[2])
    next(chains[1])
    trail_run(0, 1, cuts[2], cuts[4])
    stores.append(pltpu.make_async_copy(trail.at[0], update_hbm.at[0], update_sem.at[0]))
    stores[0].start()
    next(chains[1], None)
    trail_run(1, 1, 0, steps)
    stores.append(pltpu.make_async_copy(trail.at[1], update_hbm.at[1], update_sem.at[1]))
    stores[1].start()
    vertex_collect()
    for copy in sent:
        copy.wait_send()
    for copy in stores:
        copy.wait()


def trail_tile(count):
    return min(count, 256)


def body(dims, panel_inverse, panel_below, trail_factor, first_rhs, second_rhs, trail_rhs,
         shape_tiles, element_vertices, vertex_slot):
    nx, ny, nz = dims
    n = nx * 2 * ny * nz
    h, nb = panel_inverse.shape[3], panel_inverse.shape[4]
    angles = first_rhs.shape[3]
    count = trail_factor.shape[3]
    kind = BF16 if h % 16 == 0 else F32
    lanes = 128
    slot_count = vertex_slot.shape[0]
    widest = max(nx, ny, nz, nx + ny)
    vmem = pl.BlockSpec(memory_space=pltpu.VMEM)
    hbm = pl.BlockSpec(memory_space=pl.ANY)
    return pl.pallas_call(
        functools.partial(kernel, dims),
        out_shape=(
            jax.ShapeDtypeStruct((2, 2, 2, h, angles), BF16),
            jax.ShapeDtypeStruct(trail_rhs.shape, BF16),
            jax.ShapeDtypeStruct((3, slot_count // n), F32),
        ),
        in_specs=[vmem] * 6 + [hbm] * 3,
        out_specs=(vmem, hbm, vmem),
        scratch_shapes=[
            pltpu.VMEM(first_rhs.shape, BF16),
            pltpu.VMEM(trail_factor.shape, BF16),
            pltpu.VMEM(trail_rhs.shape, BF16),
            pltpu.VMEM(trail_rhs.shape, F32),
            pltpu.VMEM((12, nx, 2, nz, ny, h, angles), kind),
            pltpu.VMEM((n, h, lanes), kind),
            pltpu.VMEM((lanes, nb), BF16),
            pltpu.VMEM((n, h, lanes), kind),
            pltpu.VMEM((n, slot_count // n, 128), F32),
            pltpu.VMEM((n, slot_count // n, 128), F32),
            pltpu.SemaphoreType.DMA((2,)),
            pltpu.SemaphoreType.DMA((2, 2)),
            pltpu.SemaphoreType.DMA((2,)),
            pltpu.SemaphoreType.DMA((2,)),
            pltpu.SemaphoreType.DMA((2, 4, 12, widest)),
            pltpu.SemaphoreType.DMA((n,)),
            pltpu.SemaphoreType.DMA((n,)),
            pltpu.SemaphoreType.DMA((n,)),
            pltpu.SemaphoreType.DMA((n,)),
        ],
        compiler_params=pltpu.CompilerParams(
            collective_id=0, has_side_effects=True, vmem_limit_bytes=56 * 1024 * 1024
        ),
        cost_estimate=pl.CostEstimate(
            flops=32 * count * nb * angles, bytes_accessed=24 * 1024 * 1024, transcendentals=0
        ),
    )(panel_inverse, panel_below, second_rhs, shape_tiles, element_vertices.transpose(2, 0, 1),
      vertex_slot.reshape(1, slot_count), first_rhs, trail_factor, trail_rhs)


def solution(mesh):
    rows, cols = mesh.shape["row"], mesh.shape["col"]
    nx = max(rows // 2, 1)
    ny = nx if cols % nx == 0 else 1
    return jax.shard_map(
        functools.partial(body, (nx, ny, cols // ny)),
        mesh=mesh,
        in_specs=(
            P(None, None, None, ("row", "col"), None),
            P(None, None, ("row", "col"), None),
            P(None, None, None, ("row", "col"), None),
            P(),
            P(None, None, ("row", "col"), None),
            P(None, None, ("row", "col"), None),
            P(None, None, None, ("row", "col")),
            P(None, ("row", "col"), None),
            P(),
        ),
        out_specs=(
            P(None, None, None, ("row", "col"), None),
            P(None, None, ("row", "col"), None),
            P(None, ("row", "col")),
        ),
        check_vma=False,
    )
```

```python
import functools

import jax
import jax.numpy as jnp
from jax import lax
from jax.experimental import pallas as pl
from jax.experimental.pallas import tpu as pltpu
from jax.sharding import PartitionSpec as P

MESH = pl.DeviceIdType.MESH
F32 = jnp.float32
BF16 = jnp.bfloat16


def stack_rows(top, bottom):
    if top.shape[0] % 16:
        return jnp.concatenate([top.astype(F32), bottom.astype(F32)], axis=0).astype(BF16)
    return jnp.concatenate([top, bottom], axis=0)


def split_columns(parts, kind):
    h, width = parts[0].shape
    per, groups = 128 // h, width // 128
    wide = F32 if h % 16 else BF16
    rows = [jnp.concatenate([part[:, 128 * g:128 * (g + 1)] for part in parts], axis=1)
            for g in range(groups)]
    left = jnp.concatenate([row.astype(wide) for row in rows], axis=0).astype(BF16)
    source = lax.broadcasted_iota(jnp.int32, (512, per * 128), 0)
    target = lax.broadcasted_iota(jnp.int32, (512, per * 128), 1)
    shift = h.bit_length() - 1
    lane = source & 127
    goal = (lane & (h - 1)) + ((source >> 7) << shift) + ((lane >> shift) << 7)
    match = target == goal
    moved = jnp.dot(left, jnp.where(match, 1.0, 0.0).astype(BF16), preferred_element_type=F32)
    return [moved[g * h:(g + 1) * h, r * 128:(r + 1) * 128].astype(kind)
            for g in range(groups) for r in range(per)]


def kernel(dims, inv, below_in, second, shapes, corners, slots, rhs_hbm, factor_hbm, trail_hbm,
           panel_out, update_hbm, vertex_out,
           rhs, factor, trail, update, held, columns, turned, below, dense, sums,
           rhs_sem, factor_sem, trail_sem, update_sem,
           sems, column_send, column_recv, dense_send, dense_recv):
    nx, ny, nz = dims
    rows, cols = nx * 2, ny * nz
    n = rows * cols
    h = inv.shape[3]
    nb = inv.shape[4]
    angles = second.shape[3]
    steps = factor.shape[3] // trail_tile(factor.shape[3])
    tile = trail_tile(factor.shape[3])
    row, col = lax.axis_index("row"), lax.axis_index("col")
    x, core = row // 2, row % 2
    z, y = col // ny, col % ny
    me = row * cols + col
    sent = []

    loads = {}
    for s in range(2):
        loads["rhs", s] = pltpu.make_async_copy(rhs_hbm.at[s], rhs.at[s], rhs_sem.at[s])
        loads["rhs", s].start()

    barrier = pltpu.get_barrier_semaphore()

    def greet(k, carry):
        other = lax.rem(me + k, n)
        pl.semaphore_signal(barrier, inc=1, device_id=(other // cols, other % cols),
                            device_id_type=MESH)
        return carry

    lax.fori_loop(1, n, greet, 0)
    for t in range(2):
        for s in range(2):
            loads["factor", s, t] = pltpu.make_async_copy(
                factor_hbm.at[s, t], factor.at[s, t], factor_sem.at[s, t])
            loads["factor", s, t].start()
            if t == 0:
                loads["trail", s] = pltpu.make_async_copy(
                    trail_hbm.at[s], trail.at[s], trail_sem.at[s])
                loads["trail", s].start()

    def column_copy(target, source):
        return pltpu.make_async_remote_copy(
            src_ref=below.at[target], dst_ref=columns.at[source],
            send_sem=column_send.at[target], recv_sem=column_recv.at[source],
            device_id=(target // cols, target % cols), device_id_type=MESH)

    def remote(index, stage, k, region, target):
        copy = pltpu.make_async_remote_copy(
            src_ref=held.at[(index,) + region], dst_ref=held.at[(index,) + region],
            send_sem=sems.at[0, stage, index, k], recv_sem=sems.at[1, stage, index, k],
            device_id=target, device_id_type=MESH)
        return copy

    def send(index, stage, k, region, target):
        copy = remote(index, stage, k, region, target)
        copy.start()
        sent.append(copy)

    def receive(index, stage, k, region):
        remote(index, stage, k, region, (row, col)).wait_recv()

    every = slice(None)

    def spread(round_, s, make_block):
        indices = [(round_ * 2 + s) * 2 + p for p in range(2)]
        mate = (x * 2 + 1 - core, col)
        real, imag = make_block()
        for i, part in zip(indices, (real, imag)):
            held[i, x, core, z, y] = part.astype(held.dtype)
            for k in range(1, nz):
                send(i, 0, k, (x, core, z, y), (row, lax.rem(z + k, nz) * ny + y))
        yield
        for p, i in enumerate(indices):
            for k in range(1, nz):
                receive(i, 0, k, (x, core, lax.rem(z + nz - k, nz), y))
            line = (x, core, every, y)
            if p == 0:
                for k in range(1, ny):
                    send(i, 1, k, line, (row, z * ny + lax.rem(y + k, ny)))
            else:
                for k in range(1, nx):
                    send(i, 1, k, line, (lax.rem(x + k, nx) * 2 + core, col))
            send(i, 3, 0, line, mate)
        yield
        for p, i in enumerate(indices):
            if p == 0:
                got = [(x, core, every, lax.rem(y + ny - k, ny)) for k in range(1, ny)]
            else:
                got = [(lax.rem(x + nx - k, nx), core, every, y) for k in range(1, nx)]
            for k, region in enumerate(got):
                receive(i, 1, k + 1, region)
            if p == 0:
                for k in range(1, nx):
                    send(i, 2, k, (x, core), (lax.rem(x + k, nx) * 2 + core, col))
            else:
                for k in range(1, ny):
                    send(i, 2, k, (every, core, every, y), (row, z * ny + lax.rem(y + k, ny)))
            for k, region in enumerate(got):
                send(i, 3, 1 + k, region, mate)
        yield
        for p, i in enumerate(indices):
            if p == 0:
                got = [(lax.rem(x + nx - k, nx), core) for k in range(1, nx)]
            else:
                got = [(every, core, every, lax.rem(y + ny - k, ny)) for k in range(1, ny)]
            for k, region in enumerate(got):
                receive(i, 2, k + 1, region)
                base = ny if p == 0 else nx
                send(i, 3, base + k, region, mate)
        yield
        far = 1 - core
        for p, i in enumerate(indices):
            receive(i, 3, 0, (x, far, every, y))
            if p == 0:
                got = [(x, far, every, lax.rem(y + ny - k, ny)) for k in range(1, ny)]
                got += [(lax.rem(x + nx - k, nx), far) for k in range(1, nx)]
            else:
                got = [(lax.rem(x + nx - k, nx), far, every, y) for k in range(1, nx)]
                got += [(every, far, every, lax.rem(y + ny - k, ny)) for k in range(1, ny)]
            for k, region in enumerate(got):
                receive(i, 3, 1 + k, region)

    def gathered(round_, s, p):
        block = held[(round_ * 2 + s) * 2 + p]
        return block.reshape(nb, angles).astype(BF16)

    def dot(a, b):
        return jnp.dot(a, b, preferred_element_type=F32)

    def solve(s, panel, right):
        left = stack_rows(inv[s, panel, 0], inv[s, panel, 1])
        by_real, by_imag = dot(left, right[0]), dot(left, right[1])
        real = (by_real[:h] - by_imag[h:]).astype(BF16)
        imag = (by_imag[:h] + by_real[h:]).astype(BF16)
        panel_out[s, panel, 0] = real
        panel_out[s, panel, 1] = imag
        return real, imag

    def first_block(s):
        loads["rhs", s].wait()
        return solve(s, 0, (rhs[s, 0], rhs[s, 1]))

    def right_block(s):
        left = turned[2 * s * h:2 * (s + 1) * h]
        products = [dot(left, gathered(0, s, p)) for p in range(2)]
        real = products[0][:h] - products[1][h:]
        imag = products[1][:h] + products[0][h:]
        return (second[s, 0].astype(F32) - real).astype(BF16), (
            second[s, 1].astype(F32) - imag).astype(BF16)

    def second_block(s):
        return solve(s, 1, (gathered(1, s, 0), gathered(1, s, 1)))

    def trail_part(s, t, part):
        at = pl.ds(pl.multiple_of(part * tile, tile), tile)
        solved = [gathered(2 * t, s, p) for p in range(2)]
        fr, fi = factor[s, t, 0, at, :], factor[s, t, 1, at, :]
        real = dot(fr, solved[0]) - dot(fi, solved[1])
        imag = dot(fr, solved[1]) + dot(fi, solved[0])
        if t == 0:
            update[s, 0, at, :] = trail[s, 0, at, :].astype(F32) - real
            update[s, 1, at, :] = trail[s, 1, at, :].astype(F32) - imag
        else:
            trail[s, 0, at, :] = (update[s, 0, at, :] - real).astype(BF16)
            trail[s, 1, at, :] = (update[s, 1, at, :] - imag).astype(BF16)

    def trail_run(s, t, first, last):
        if first == 0:
            loads["factor", s, t].wait()
            if t == 0:
                loads["trail", s].wait()

        def step(part, carry):
            trail_part(s, t, part)
            return carry

        lax.fori_loop(first, last, step, 0)

    def chain(s):
        yield from spread(0, s, lambda: firsts[s])
        yield from spread(1, s, lambda: right_block(s))
        yield from spread(2, s, lambda: second_block(s))

    def vertex_copy(target, source):
        return pltpu.make_async_remote_copy(
            src_ref=dense.at[target], dst_ref=sums.at[source],
            send_sem=dense_send.at[target], recv_sem=dense_recv.at[source],
            device_id=(target // cols, target % cols), device_id_type=MESH)

    def vertex_partials(t):
        fr, fi = panel_out[0, t, 0].astype(F32), panel_out[0, t, 1].astype(F32)
        ar, ai = panel_out[1, t, 0].astype(F32), panel_out[1, t, 1].astype(F32)
        ones = jnp.ones((8, angles), F32)

        def over_angles(values):
            return lax.dot_general(ones, values, (((1,), (1,)), ((), ())),
                                   precision=lax.Precision.HIGHEST,
                                   preferred_element_type=F32)[:1]

        real, imag = over_angles(fr * ar - fi * ai), over_angles(fr * ai + fi * ar)
        count = slots.shape[1]
        place = lax.broadcasted_iota(jnp.int32, (count, h), 0)
        owner = jnp.broadcast_to(slots[...].astype(F32), (8, count)).T[:, :1]
        total = None
        for c in range(3):
            named = corners[c, t:t + 1, :] == place
            slot = jnp.sum(jnp.where(named, owner, 0.0), axis=0, keepdims=True)
            hot = jnp.where(slot == place.astype(F32), 1.0, 0.0)
            at = pl.ds(3 * c, 3)
            values = shapes[1, at, t, :] * imag - shapes[0, at, t, :] * real
            values = jnp.concatenate([values, jnp.zeros((125, h), F32)], axis=0)
            term = lax.dot_general(hot, values, (((1,), (1,)), ((), ())),
                                   precision=lax.Precision.HIGHEST,
                                   preferred_element_type=F32)
            total = term if total is None else total + term
        return total

    def vertex_send():
        total = vertex_partials(0) + vertex_partials(1)
        dense[...] = total.reshape(dense.shape)
        sums[me] = dense[me]

        def start(k, carry):
            vertex_copy(lax.rem(me + k, n), me).start()
            return carry

        lax.fori_loop(1, n, start, 0)

    def vertex_collect():
        def wait(k, carry):
            vertex_copy(lax.rem(me + k, n), lax.rem(me + n - k, n)).wait()
            return carry

        lax.fori_loop(1, n, wait, 0)
        vertex_out[...] = jnp.sum(sums[...], axis=0).T[:3]

    firsts = [first_block(s) for s in range(2)]
    pl.semaphore_wait(barrier, n - 1)

    chains = [chain(0), chain(1)]
    next(chains[0])
    parts = [below_in[i, p] for i in range(2) for p in range(2)]
    for d, block in enumerate(split_columns(parts, below.dtype)):
        below[d] = block
    columns[me] = below[me]

    def scatter(k, carry):
        column_copy(lax.rem(me + k, n), me).start()
        return carry

    lax.fori_loop(1, n, scatter, 0)
    next(chains[0])
    next(chains[1])
    next(chains[0])
    next(chains[0])
    next(chains[1])

    def collect(k, carry):
        column_copy(lax.rem(me + k, n), lax.rem(me + n - k, n)).wait()
        return carry

    lax.fori_loop(1, n, collect, 0)
    turned[...] = columns[...].astype(F32).reshape(nb, columns.shape[2]).T.astype(BF16)
    cuts = [steps * k // 4 for k in range(5)]
    for round_ in range(2):
        next(chains[0])
        next(chains[1])
        trail_run(round_, 0, cuts[0], cuts[2])
        next(chains[0])
        next(chains[1])
        next(chains[0])
        next(chains[1])
        trail_run(round_, 0, cuts[2], cuts[4])
        next(chains[0])
        next(chains[1])
        if round_ == 1:
            vertex_send()
    stores = []
    next(chains[0], None)
    next(chains[1])
    next(chains[1])
    trail_run(0, 1, 0, steps)
    stores.append(pltpu.make_async_copy(trail.at[0], update_hbm.at[0], update_sem.at[0]))
    stores[0].start()
    next(chains[1], None)
    trail_run(1, 1, 0, steps)
    stores.append(pltpu.make_async_copy(trail.at[1], update_hbm.at[1], update_sem.at[1]))
    stores[1].start()
    vertex_collect()
    for copy in sent:
        copy.wait_send()
    for copy in stores:
        copy.wait()


def trail_tile(count):
    return min(count, 256)


def body(dims, panel_inverse, panel_below, trail_factor, first_rhs, second_rhs, trail_rhs,
         shape_tiles, element_vertices, vertex_slot):
    nx, ny, nz = dims
    n = nx * 2 * ny * nz
    h, nb = panel_inverse.shape[3], panel_inverse.shape[4]
    angles = first_rhs.shape[3]
    count = trail_factor.shape[3]
    kind = BF16 if h % 16 == 0 else F32
    lanes = 128
    slot_count = vertex_slot.shape[0]
    widest = max(nx, ny, nz, nx + ny)
    vmem = pl.BlockSpec(memory_space=pltpu.VMEM)
    hbm = pl.BlockSpec(memory_space=pl.ANY)
    return pl.pallas_call(
        functools.partial(kernel, dims),
        out_shape=(
            jax.ShapeDtypeStruct((2, 2, 2, h, angles), BF16),
            jax.ShapeDtypeStruct(trail_rhs.shape, BF16),
            jax.ShapeDtypeStruct((3, slot_count // n), F32),
        ),
        in_specs=[vmem] * 6 + [hbm] * 3,
        out_specs=(vmem, hbm, vmem),
        scratch_shapes=[
            pltpu.VMEM(first_rhs.shape, BF16),
            pltpu.VMEM(trail_factor.shape, BF16),
            pltpu.VMEM(trail_rhs.shape, BF16),
            pltpu.VMEM(trail_rhs.shape, F32),
            pltpu.VMEM((12, nx, 2, nz, ny, h, angles), kind),
            pltpu.VMEM((n, h, lanes), kind),
            pltpu.VMEM((lanes, nb), BF16),
            pltpu.VMEM((n, h, lanes), kind),
            pltpu.VMEM((n, slot_count // n, 128), F32),
            pltpu.VMEM((n, slot_count // n, 128), F32),
            pltpu.SemaphoreType.DMA((2,)),
            pltpu.SemaphoreType.DMA((2, 2)),
            pltpu.SemaphoreType.DMA((2,)),
            pltpu.SemaphoreType.DMA((2,)),
            pltpu.SemaphoreType.DMA((2, 4, 12, widest)),
            pltpu.SemaphoreType.DMA((n,)),
            pltpu.SemaphoreType.DMA((n,)),
            pltpu.SemaphoreType.DMA((n,)),
            pltpu.SemaphoreType.DMA((n,)),
        ],
        compiler_params=pltpu.CompilerParams(
            collective_id=0, has_side_effects=True, vmem_limit_bytes=56 * 1024 * 1024
        ),
        cost_estimate=pl.CostEstimate(
            flops=32 * count * nb * angles, bytes_accessed=24 * 1024 * 1024, transcendentals=0
        ),
    )(panel_inverse, panel_below, second_rhs, shape_tiles, element_vertices.transpose(2, 0, 1),
      vertex_slot.reshape(1, slot_count), first_rhs, trail_factor, trail_rhs)


def solution(mesh):
    rows, cols = mesh.shape["row"], mesh.shape["col"]
    nx = max(rows // 2, 1)
    ny = nx if cols % nx == 0 else 1
    return jax.shard_map(
        functools.partial(body, (nx, ny, cols // ny)),
        mesh=mesh,
        in_specs=(
            P(None, None, None, ("row", "col"), None),
            P(None, None, ("row", "col"), None),
            P(None, None, None, ("row", "col"), None),
            P(),
            P(None, None, ("row", "col"), None),
            P(None, None, ("row", "col"), None),
            P(None, None, None, ("row", "col")),
            P(None, ("row", "col"), None),
            P(),
        ),
        out_specs=(
            P(None, None, None, ("row", "col"), None),
            P(None, None, ("row", "col"), None),
            P(None, ("row", "col")),
        ),
        check_vma=False,
    )
```

```python
import functools

import jax
import jax.numpy as jnp
from jax import lax
from jax.experimental import pallas as pl
from jax.experimental.pallas import tpu as pltpu
from jax.sharding import PartitionSpec as P

MESH = pl.DeviceIdType.MESH
F32 = jnp.float32
BF16 = jnp.bfloat16


def stack_rows(top, bottom):
    if top.shape[0] % 16:
        return jnp.concatenate([top.astype(F32), bottom.astype(F32)], axis=0).astype(BF16)
    return jnp.concatenate([top, bottom], axis=0)


def split_columns(parts, kind):
    h, width = parts[0].shape
    per, groups = 128 // h, width // 128
    wide = F32 if h % 16 else BF16
    rows = [jnp.concatenate([part[:, 128 * g:128 * (g + 1)] for part in parts], axis=1)
            for g in range(groups)]
    left = jnp.concatenate([row.astype(wide) for row in rows], axis=0).astype(BF16)
    source = lax.broadcasted_iota(jnp.int32, (512, per * 128), 0)
    target = lax.broadcasted_iota(jnp.int32, (512, per * 128), 1)
    shift = h.bit_length() - 1
    lane = source & 127
    goal = (lane & (h - 1)) + ((source >> 7) << shift) + ((lane >> shift) << 7)
    match = target == goal
    moved = jnp.dot(left, jnp.where(match, 1.0, 0.0).astype(BF16), preferred_element_type=F32)
    return [moved[g * h:(g + 1) * h, r * 128:(r + 1) * 128].astype(kind)
            for g in range(groups) for r in range(per)]


def kernel(dims, inv, below_in, second, shapes, corners, slots, rhs_hbm, factor_hbm, trail_hbm,
           panel_out, update_hbm, vertex_out,
           rhs, factor, trail, update, held, columns, turned, below, dense, sums,
           rhs_sem, factor_sem, trail_sem, update_sem,
           sems, column_send, column_recv, dense_send, dense_recv):
    nx, ny, nz = dims
    rows, cols = nx * 2, ny * nz
    n = rows * cols
    h = inv.shape[3]
    nb = inv.shape[4]
    angles = second.shape[3]
    steps = factor.shape[3] // trail_tile(factor.shape[3])
    tile = trail_tile(factor.shape[3])
    row, col = lax.axis_index("row"), lax.axis_index("col")
    x, core = row // 2, row % 2
    z, y = col // ny, col % ny
    me = row * cols + col
    sent = []

    loads = {}
    for s in range(2):
        loads["rhs", s] = pltpu.make_async_copy(rhs_hbm.at[s], rhs.at[s], rhs_sem.at[s])
        loads["rhs", s].start()

    barrier = pltpu.get_barrier_semaphore()

    def greet(k, carry):
        other = lax.rem(me + k, n)
        pl.semaphore_signal(barrier, inc=1, device_id=(other // cols, other % cols),
                            device_id_type=MESH)
        return carry

    lax.fori_loop(1, n, greet, 0)
    for t in range(2):
        for s in range(2):
            loads["factor", s, t] = pltpu.make_async_copy(
                factor_hbm.at[s, t], factor.at[s, t], factor_sem.at[s, t])
            loads["factor", s, t].start()
            if t == 0:
                loads["trail", s] = pltpu.make_async_copy(
                    trail_hbm.at[s], trail.at[s], trail_sem.at[s])
                loads["trail", s].start()

    def column_copy(target, source):
        return pltpu.make_async_remote_copy(
            src_ref=below.at[target], dst_ref=columns.at[source],
            send_sem=column_send.at[target], recv_sem=column_recv.at[source],
            device_id=(target // cols, target % cols), device_id_type=MESH)

    def remote(index, stage, k, region, target):
        copy = pltpu.make_async_remote_copy(
            src_ref=held.at[(index,) + region], dst_ref=held.at[(index,) + region],
            send_sem=sems.at[0, stage, index, k], recv_sem=sems.at[1, stage, index, k],
            device_id=target, device_id_type=MESH)
        return copy

    def send(index, stage, k, region, target):
        copy = remote(index, stage, k, region, target)
        copy.start()
        sent.append(copy)

    def receive(index, stage, k, region):
        remote(index, stage, k, region, (row, col)).wait_recv()

    every = slice(None)

    def spread(round_, s, make_block):
        indices = [(round_ * 2 + s) * 2 + p for p in range(2)]
        mate = (x * 2 + 1 - core, col)
        real, imag = make_block()
        for i, part in zip(indices, (real, imag)):
            held[i, x, core, z, y] = part.astype(held.dtype)
            for k in range(1, nz):
                send(i, 0, k, (x, core, z, y), (row, lax.rem(z + k, nz) * ny + y))
        yield
        plane = [(a, b) for a in range(nx) for b in range(ny) if (a, b) != (0, 0)]
        for i in indices:
            for k in range(1, nz):
                receive(i, 0, k, (x, core, lax.rem(z + nz - k, nz), y))
            line = (x, core, every, y)
            for k, (a, b) in enumerate(plane):
                send(i, 1, k, line, (lax.rem(x + a, nx) * 2 + core, z * ny + lax.rem(y + b, ny)))
            send(i, 2, 0, line, mate)
        yield
        for i in indices:
            for k, (a, b) in enumerate(plane):
                line = (lax.rem(x + nx - a, nx), core, every, lax.rem(y + ny - b, ny))
                receive(i, 1, k, line)
                send(i, 2, 1 + k, line, mate)
        yield
        for i in indices:
            receive(i, 2, 0, (x, 1 - core, every, y))
            for k, (a, b) in enumerate(plane):
                line = (lax.rem(x + nx - a, nx), 1 - core, every, lax.rem(y + ny - b, ny))
                receive(i, 2, 1 + k, line)

    def gathered(round_, s, p):
        block = held[(round_ * 2 + s) * 2 + p]
        return block.reshape(nb, angles).astype(BF16)

    def dot(a, b):
        return jnp.dot(a, b, preferred_element_type=F32)

    def solve(s, panel, right):
        left = stack_rows(inv[s, panel, 0], inv[s, panel, 1])
        by_real, by_imag = dot(left, right[0]), dot(left, right[1])
        real = (by_real[:h] - by_imag[h:]).astype(BF16)
        imag = (by_imag[:h] + by_real[h:]).astype(BF16)
        panel_out[s, panel, 0] = real
        panel_out[s, panel, 1] = imag
        return real, imag

    def first_block(s):
        loads["rhs", s].wait()
        return solve(s, 0, (rhs[s, 0], rhs[s, 1]))

    def right_block(s):
        left = turned[2 * s * h:2 * (s + 1) * h]
        products = [dot(left, gathered(0, s, p)) for p in range(2)]
        real = products[0][:h] - products[1][h:]
        imag = products[1][:h] + products[0][h:]
        return (second[s, 0].astype(F32) - real).astype(BF16), (
            second[s, 1].astype(F32) - imag).astype(BF16)

    def second_block(s):
        return solve(s, 1, (gathered(1, s, 0), gathered(1, s, 1)))

    def trail_part(s, t, part):
        at = pl.ds(part * tile, tile)
        solved = [gathered(2 * t, s, p) for p in range(2)]
        fr, fi = factor[s, t, 0, at, :], factor[s, t, 1, at, :]
        real = dot(fr, solved[0]) - dot(fi, solved[1])
        imag = dot(fr, solved[1]) + dot(fi, solved[0])
        if t == 0:
            update[s, 0, at, :] = trail[s, 0, at, :].astype(F32) - real
            update[s, 1, at, :] = trail[s, 1, at, :].astype(F32) - imag
        else:
            trail[s, 0, at, :] = (update[s, 0, at, :] - real).astype(BF16)
            trail[s, 1, at, :] = (update[s, 1, at, :] - imag).astype(BF16)

    def trail_run(s, t, first, last):
        if first == 0:
            loads["factor", s, t].wait()
            if t == 0:
                loads["trail", s].wait()
        for part in range(first, last):
            trail_part(s, t, part)

    def chain(s):
        yield from spread(0, s, lambda: firsts[s])
        yield from spread(1, s, lambda: right_block(s))
        yield from spread(2, s, lambda: second_block(s))

    def vertex_copy(target, source):
        return pltpu.make_async_remote_copy(
            src_ref=dense.at[target], dst_ref=sums.at[source],
            send_sem=dense_send.at[target], recv_sem=dense_recv.at[source],
            device_id=(target // cols, target % cols), device_id_type=MESH)

    def vertex_partials(t):
        fr, fi = panel_out[0, t, 0].astype(F32), panel_out[0, t, 1].astype(F32)
        ar, ai = panel_out[1, t, 0].astype(F32), panel_out[1, t, 1].astype(F32)
        ones = jnp.ones((8, angles), F32)

        def over_angles(values):
            return lax.dot_general(ones, values, (((1,), (1,)), ((), ())),
                                   precision=lax.Precision.HIGHEST,
                                   preferred_element_type=F32)[:1]

        real, imag = over_angles(fr * ar - fi * ai), over_angles(fr * ai + fi * ar)
        count = slots.shape[1]
        place = lax.broadcasted_iota(jnp.int32, (count, h), 0)
        owner = jnp.broadcast_to(slots[...].astype(F32), (8, count)).T[:, :1]
        total = None
        for c in range(3):
            named = corners[c, t:t + 1, :] == place
            slot = jnp.sum(jnp.where(named, owner, 0.0), axis=0, keepdims=True)
            hot = jnp.where(slot == place.astype(F32), 1.0, 0.0)
            at = pl.ds(3 * c, 3)
            values = shapes[1, at, t, :] * imag - shapes[0, at, t, :] * real
            values = jnp.concatenate([values, jnp.zeros((125, h), F32)], axis=0)
            term = lax.dot_general(hot, values, (((1,), (1,)), ((), ())),
                                   precision=lax.Precision.HIGHEST,
                                   preferred_element_type=F32)
            total = term if total is None else total + term
        return total

    def vertex_send():
        total = vertex_partials(0) + vertex_partials(1)
        dense[...] = total.reshape(dense.shape)
        sums[me] = dense[me]

        def start(k, carry):
            vertex_copy(lax.rem(me + k, n), me).start()
            return carry

        lax.fori_loop(1, n, start, 0)

    def vertex_collect():
        def wait(k, carry):
            vertex_copy(lax.rem(me + k, n), lax.rem(me + n - k, n)).wait()
            return carry

        lax.fori_loop(1, n, wait, 0)
        vertex_out[...] = jnp.sum(sums[...], axis=0).T[:3]

    firsts = [first_block(s) for s in range(2)]
    pl.semaphore_wait(barrier, n - 1)

    chains = [chain(0), chain(1)]
    next(chains[0])
    parts = [below_in[i, p] for i in range(2) for p in range(2)]
    for d, block in enumerate(split_columns(parts, below.dtype)):
        below[d] = block
    columns[me] = below[me]

    def scatter(k, carry):
        column_copy(lax.rem(me + k, n), me).start()
        return carry

    lax.fori_loop(1, n, scatter, 0)
    next(chains[0])
    next(chains[1])
    next(chains[0])
    next(chains[1])

    def collect(k, carry):
        column_copy(lax.rem(me + k, n), lax.rem(me + n - k, n)).wait()
        return carry

    lax.fori_loop(1, n, collect, 0)
    turned[...] = columns[...].astype(F32).reshape(nb, columns.shape[2]).T.astype(BF16)
    cuts = [steps * k // 4 for k in range(5)]
    for round_ in range(2):
        next(chains[0])
        trail_run(round_, 0, cuts[0], cuts[1])
        next(chains[1])
        next(chains[0])
        trail_run(round_, 0, cuts[1], cuts[2])
        next(chains[1])
        trail_run(round_, 0, cuts[2], cuts[3])
        next(chains[0])
        next(chains[1])
        if round_ == 1:
            vertex_send()
        trail_run(round_, 0, cuts[3], cuts[4])
    stores = []
    next(chains[0], None)
    trail_run(0, 1, cuts[0], cuts[2])
    next(chains[1])
    trail_run(0, 1, cuts[2], cuts[4])
    stores.append(pltpu.make_async_copy(trail.at[0], update_hbm.at[0], update_sem.at[0]))
    stores[0].start()
    next(chains[1], None)
    trail_run(1, 1, 0, steps)
    stores.append(pltpu.make_async_copy(trail.at[1], update_hbm.at[1], update_sem.at[1]))
    stores[1].start()
    vertex_collect()
    for copy in sent:
        copy.wait_send()
    for copy in stores:
        copy.wait()


def trail_tile(count):
    return min(count, 256)


def body(dims, panel_inverse, panel_below, trail_factor, first_rhs, second_rhs, trail_rhs,
         shape_tiles, element_vertices, vertex_slot):
    nx, ny, nz = dims
    n = nx * 2 * ny * nz
    h, nb = panel_inverse.shape[3], panel_inverse.shape[4]
    angles = first_rhs.shape[3]
    count = trail_factor.shape[3]
    kind = BF16 if h % 16 == 0 else F32
    lanes = 128
    slot_count = vertex_slot.shape[0]
    widest = max(nz, nx * ny)
    vmem = pl.BlockSpec(memory_space=pltpu.VMEM)
    hbm = pl.BlockSpec(memory_space=pl.ANY)
    return pl.pallas_call(
        functools.partial(kernel, dims),
        out_shape=(
            jax.ShapeDtypeStruct((2, 2, 2, h, angles), BF16),
            jax.ShapeDtypeStruct(trail_rhs.shape, BF16),
            jax.ShapeDtypeStruct((3, slot_count // n), F32),
        ),
        in_specs=[vmem] * 6 + [hbm] * 3,
        out_specs=(vmem, hbm, vmem),
        scratch_shapes=[
            pltpu.VMEM(first_rhs.shape, BF16),
            pltpu.VMEM(trail_factor.shape, BF16),
            pltpu.VMEM(trail_rhs.shape, BF16),
            pltpu.VMEM(trail_rhs.shape, F32),
            pltpu.VMEM((12, nx, 2, nz, ny, h, angles), kind),
            pltpu.VMEM((n, h, lanes), kind),
            pltpu.VMEM((lanes, nb), BF16),
            pltpu.VMEM((n, h, lanes), kind),
            pltpu.VMEM((n, slot_count // n, 128), F32),
            pltpu.VMEM((n, slot_count // n, 128), F32),
            pltpu.SemaphoreType.DMA((2,)),
            pltpu.SemaphoreType.DMA((2, 2)),
            pltpu.SemaphoreType.DMA((2,)),
            pltpu.SemaphoreType.DMA((2,)),
            pltpu.SemaphoreType.DMA((2, 3, 12, widest)),
            pltpu.SemaphoreType.DMA((n,)),
            pltpu.SemaphoreType.DMA((n,)),
            pltpu.SemaphoreType.DMA((n,)),
            pltpu.SemaphoreType.DMA((n,)),
        ],
        compiler_params=pltpu.CompilerParams(
            collective_id=0, has_side_effects=True, vmem_limit_bytes=56 * 1024 * 1024
        ),
        cost_estimate=pl.CostEstimate(
            flops=32 * count * nb * angles, bytes_accessed=24 * 1024 * 1024, transcendentals=0
        ),
    )(panel_inverse, panel_below, second_rhs, shape_tiles, element_vertices.transpose(2, 0, 1),
      vertex_slot.reshape(1, slot_count), first_rhs, trail_factor, trail_rhs)


def solution(mesh):
    rows, cols = mesh.shape["row"], mesh.shape["col"]
    nx = max(rows // 2, 1)
    ny = nx if cols % nx == 0 else 1
    return jax.shard_map(
        functools.partial(body, (nx, ny, cols // ny)),
        mesh=mesh,
        in_specs=(
            P(None, None, None, ("row", "col"), None),
            P(None, None, ("row", "col"), None),
            P(None, None, None, ("row", "col"), None),
            P(),
            P(None, None, ("row", "col"), None),
            P(None, None, ("row", "col"), None),
            P(None, None, None, ("row", "col")),
            P(None, ("row", "col"), None),
            P(),
        ),
        out_specs=(
            P(None, None, None, ("row", "col"), None),
            P(None, None, ("row", "col"), None),
            P(None, ("row", "col")),
        ),
        check_vma=False,
    )
```
